32 devices in a mesh: dp: 4 (over y, x), tile: 8 (over z, core).
Axes of the slice: x: 2, y: 2, z: 4, core: 2. Of those that a mesh axis runs over, the one named last changes fastest.
Arguments:
- features: bfloat16 [4, 4, 64, 8, 192], P('dp', None, 'tile'), may hold values from -40 to 40
- out_grad: bfloat16 [4, 4, 64, 8, 192], P('dp', None, 'tile'), may hold values from -6 to 6
- weight: bfloat16 [192, 27, 192], P('tile', None, 'dp'), may hold values from -0.078125 to 0.078125
- bias: float32 [192], replicated, may hold values from -3 to 3
- gamma: float32 [192], replicated, may hold values from 0.1 to 1.9
- beta: float32 [192], replicated, may hold values from -3 to 3
- tile_clip: int32 [4, 8], P('dp'), may hold values from 0 to 6, as said below
- tile_rows: int32 [4, 8], P('dp'), may hold values from 1 to 8, as said below
- clip_cols: int32 [4, 8], P('dp'), may hold values from 4 to 8, as said below
- clip_start: int32 [4, 8], P('dp'), may hold values from 0 to 2, as said below
Outputs:
- conv_out: bfloat16 [4, 4, 64, 8, 192], P('dp', None, 'tile')
- input_grad: bfloat16 [4, 4, 64, 8, 192], P('dp', None, 'tile')
- weight_grad: float32 [192, 27, 192], P('tile', None, 'dp')
The draws below stay inside these ranges and needn't reach their ends.
Inputs may be any that keep to these rules, and one draw needn't show every extreme that they name: `tile_clip`: in each batch clip numbers start at 0 at tile 0 and rise by 0 or 1 from one tile to the next, so a clip's tiles are consecutive; tiles 0 and 1 share a clip. `tile_rows`: 8 for every tile but the last of its clip, which may have fewer. `clip_cols`: entries past a batch's last clip are not read. `clip_start`: entries past a batch's last clip are not read.
All inputs are finite; a program needn't handle non-finite values.
Results may differ from the reference program's by a relative error of at most 0.0039.
Values may be sent and summed in bfloat16 or wider, within the bound.
No kernel may reach another device: no remote copies, remote signals or barrier semaphores. Data moves between devices by JAX's collectives and lax.ppermute only.
A program may use at most 64 MiB of HBM per device.

```python
import jax
import jax.numpy as jnp
from jax import lax

C = 192
G = 32
F = 4
TH = 8
TW = 8
ROWS = 64
N_DP = 4
N_TILE = 8


def layout(key):
    flags = (jax.random.randint(jax.random.fold_in(key, 11), (N_DP, N_TILE), 0, 3) == 0).astype(jnp.int32)
    busiest = jax.random.randint(jax.random.fold_in(key, 13), (), 0, N_DP)
    batch_index = jnp.arange(N_DP, dtype=jnp.int32)[:, None]
    flags = jnp.where(batch_index == busiest, 1, flags).astype(jnp.int32)
    flags = flags.at[:, 0].set(1).at[:, 1].set(0)
    clips = jnp.cumsum(flags, axis=1) - 1
    last_tile = jnp.concatenate([flags[:, 1:], jnp.ones((N_DP, 1), jnp.int32)], axis=1)
    partial_rows = jax.random.randint(jax.random.fold_in(key, 12), (N_DP, N_TILE), 1, TH + 1)
    rows = jnp.where(last_tile == 1, partial_rows, TH).astype(jnp.int32)
    return (clips.astype(jnp.int32), rows)


def draw_tile_clip(key, part):
    return layout(key)[0]


def draw_tile_rows(key, part):
    return layout(key)[1]


def draw_clip_cols(key, part):
    values = jax.random.randint(jax.random.fold_in(key, 21), (N_DP, N_TILE), TW // 2, TW + 1)
    return values.at[:, 0].set(TW).at[:, 1].set(TW // 2).astype(jnp.int32)


def draw_clip_start(key, part):
    values = jax.random.randint(jax.random.fold_in(key, 31), (N_DP, N_TILE), 0, 3)
    return values.at[:, 0].set(0).at[:, 1].set(2).astype(jnp.int32)


def draw_features(key, part):
    shape = (N_DP, F, TH * N_TILE, TW, C)
    row_scale = jnp.exp(jax.random.uniform(jax.random.fold_in(key, 41), (N_DP, F, TH * N_TILE, 1, 1), minval=-1.15, maxval=1.15))
    channel_scale = jnp.exp(jax.random.uniform(jax.random.fold_in(key, 42), (C,), minval=-1.15, maxval=1.15))
    base = jnp.clip(jax.random.normal(jax.random.fold_in(key, 45), shape), -4.0, 4.0)
    return (base * row_scale * channel_scale).astype(jnp.bfloat16)


def level_of(rng, extent, shards, smallest, high):
    factor_of, own = 1.0, jax.random.fold_in(rng, 6)
    for dim, parts in shards:
        draws = jnp.exp(jax.random.uniform(jax.random.fold_in(own, dim), (parts,), jnp.float32, smallest / len(shards), high / len(shards)))
        factor_of = factor_of * jnp.repeat(draws, extent[dim] // parts).reshape([-1 if axis == dim else 1 for axis in range(len(extent))])
    return factor_of


def gaussian(rng, dims, width, limit, cuts=(), held_as=jnp.bfloat16):
    drawn = width * jax.random.normal(rng, dims, jnp.float32)
    if cuts:
        drawn = drawn * level_of(rng, dims, cuts, -0.22, 0.18)
    return jnp.clip(drawn, -limit, limit).astype(held_as)


def setup_inputs(seed: int = 0) -> dict:
    keys = jax.random.split(jax.random.key(seed), 11)
    return {
        "features": draw_features(jax.random.fold_in(keys[10], 71), 0),
        "out_grad": gaussian(keys[1], (N_DP, F, ROWS, TW, C), 1.0, 6.0, ((0, 4), (2, 8))),
        "weight": gaussian(keys[2], (C, 27, C), (27 * C) ** -0.5, 0.078125, ((0, 8), (2, 4))),
        "bias": gaussian(keys[3], (C,), 0.5, 3.0, (), jnp.float32),
        "gamma": jnp.clip(1.0 + 0.18 * jax.random.normal(keys[4], (C,), jnp.float32), 0.1, 1.9),
        "beta": gaussian(keys[5], (C,), 0.5, 3.0, (), jnp.float32),
        "tile_clip": draw_tile_clip(jax.random.fold_in(keys[10], 71), 0),
        "tile_rows": draw_tile_rows(jax.random.fold_in(keys[10], 71), 0),
        "clip_cols": draw_clip_cols(jax.random.fold_in(keys[10], 71), 0),
        "clip_start": draw_clip_start(jax.random.fold_in(keys[10], 71), 0),
    }


EPSILON = 1e-05

def with_rims(tiled, keep_above, keep_below):
    zero_row = jnp.zeros_like(tiled[:1, :, :1])
    above = jnp.concatenate([zero_row, tiled[:-1, :, -1:]], axis=0) * keep_above[:, None, None, None, None]
    below = jnp.concatenate([tiled[1:, :, :1], zero_row], axis=0) * keep_below[:, None, None, None, None]
    return jnp.concatenate([above, tiled, below], axis=2)

def reference(features, out_grad, weight, bias, gamma, beta, tile_clip, tile_rows, clip_cols, clip_start):
    group_size = C // G
    tiles = jnp.arange(N_TILE, dtype=jnp.int32)
    frame_index = jnp.arange(F, dtype=jnp.int32)[None, :, None, None]
    row_index = jnp.arange(TH, dtype=jnp.int32)[None, None, :, None]
    col_index = jnp.arange(TW, dtype=jnp.int32)[None, None, None, :]
    offsets = [(a, b, e) for a in range(3) for b in range(3) for e in range(3)]

    def tile_step(total, item):
        hidden_pad, grad_pad = item
        grad_centre = grad_pad[:F, 1:TH + 1, 1:TW + 1].reshape(-1, C)
        conv_sum = jnp.zeros((F * TH * TW, C), jnp.float32)
        hidden_grad = jnp.zeros((F * TH * TW, C), jnp.float32)
        pieces = []
        for tap, (a, b, e) in enumerate(offsets):
            hidden_slice = hidden_pad[a:a + F, b:b + TH, e:e + TW].reshape(-1, C)
            grad_slice = grad_pad[2 - a:2 - a + F, 2 - b:2 - b + TH, 2 - e:2 - e + TW].reshape(-1, C)
            tap_weight = weight[:, tap, :]
            conv_sum = conv_sum + jnp.dot(hidden_slice, tap_weight, preferred_element_type=jnp.float32)
            hidden_grad = hidden_grad + jnp.dot(grad_slice, tap_weight.T, preferred_element_type=jnp.float32)
            pieces.append(jnp.dot(hidden_slice.T, grad_centre, preferred_element_type=jnp.float32))
        return (total + jnp.stack(pieces, axis=1), (conv_sum, hidden_grad))

    def row_step(total, item):
        feats, grads_in, clips, rows, cols_table, start_table = item
        tiled = feats.reshape(F, N_TILE, TH, TW, C).transpose(1, 0, 2, 3, 4)
        grad_tiled = grads_in.reshape(F, N_TILE, TH, TW, C).transpose(1, 0, 2, 3, 4)
        cols = jnp.take(cols_table, clips)
        first = jnp.take(start_table, clips)
        valid = ((frame_index >= first[:, None, None, None]) & (row_index < rows[:, None, None, None]) & (col_index < cols[:, None, None, None])).astype(jnp.float32)[..., None]
        same = clips[:, None] == clips[None, :]
        clip_rows = lax.optimization_barrier(jnp.sum(jnp.where(same, rows[None, :], 0), axis=1))
        counted = ((F - first) * cols * clip_rows * group_size).astype(jnp.float32)[:, None]

        def clip_total(part):
            return lax.optimization_barrier(jnp.sum(jnp.where(same[:, :, None], part[None, :, :], 0.0), axis=1))
        masked = tiled.astype(jnp.float32) * valid
        grouped = masked.reshape(N_TILE, F, TH, TW, G, group_size)
        first_sum = lax.optimization_barrier(jnp.sum(grouped, axis=(1, 2, 3, 5)))
        square_sum = lax.optimization_barrier(jnp.sum(grouped * grouped, axis=(1, 2, 3, 5)))
        mean_value = clip_total(first_sum) / counted
        variance = clip_total(square_sum) / counted - mean_value * mean_value
        inv_std = lax.rsqrt(variance + EPSILON)
        expand = (slice(None), None, None, None, slice(None), None)
        normed_groups = (grouped - mean_value[expand]) * inv_std[expand]
        normed = normed_groups.reshape(N_TILE, F, TH, TW, C)
        activation = normed * gamma + beta
        sigmoid_act = jax.nn.sigmoid(activation)
        hidden = (activation * sigmoid_act * valid).astype(jnp.bfloat16)
        grad_masked = (grad_tiled.astype(jnp.float32) * valid).astype(jnp.bfloat16)
        keep_above = ((tiles > 0) & (jnp.roll(clips, 1) == clips)).astype(jnp.bfloat16)
        keep_below = ((tiles < N_TILE - 1) & (jnp.roll(clips, -1) == clips)).astype(jnp.bfloat16)
        hidden_pad = jnp.pad(with_rims(hidden, keep_above, keep_below), ((0, 0), (2, 0), (0, 0), (1, 1), (0, 0)))
        grad_pad = jnp.pad(with_rims(grad_masked, keep_above, keep_below), ((0, 0), (0, 2), (0, 0), (1, 1), (0, 0)))
        total, (conv_sum, hidden_grad) = lax.scan(tile_step, total, (hidden_pad, grad_pad))
        conv_sum = conv_sum.reshape(N_TILE, F, TH, TW, C)
        hidden_grad = hidden_grad.reshape(N_TILE, F, TH, TW, C)
        conv_out = ((conv_sum + bias) * valid).astype(jnp.bfloat16)
        dnormed = hidden_grad * valid * sigmoid_act * (1.0 + activation * (1.0 - sigmoid_act)) * gamma
        dgroups = dnormed.reshape(N_TILE, F, TH, TW, G, group_size)
        first_total = clip_total(lax.optimization_barrier(jnp.sum(dgroups, axis=(1, 2, 3, 5)))) / counted
        second_total = clip_total(lax.optimization_barrier(jnp.sum(dgroups * normed_groups, axis=(1, 2, 3, 5)))) / counted
        input_groups = inv_std[expand] * (dgroups - first_total[expand] - normed_groups * second_total[expand])
        input_grad = (input_groups.reshape(N_TILE, F, TH, TW, C) * valid).astype(jnp.bfloat16)
        conv_row = conv_out.transpose(1, 0, 2, 3, 4).reshape(F, N_TILE * TH, TW, C)
        grad_row = input_grad.transpose(1, 0, 2, 3, 4).reshape(F, N_TILE * TH, TW, C)
        return (total, (conv_row, grad_row))
    start_total = jnp.zeros((C, 27, C), jnp.float32)
    weight_grad, (conv_out, input_grad) = lax.scan(row_step, start_total, (features, out_grad, tile_clip, tile_rows, clip_cols, clip_start))
    return (conv_out, input_grad, weight_grad)
```

```python
import functools

import jax
import jax.numpy as jnp
from jax import lax
from jax.experimental import pallas as pl
from jax.experimental.pallas import tpu as pltpu
from jax.sharding import PartitionSpec as P

G = 32
EPSILON = 1e-05
WIDE = 256
HALF_TAPS = 14
FRAMES, HEIGHT, WIDTH = 4, 8, 8
CELLS = FRAMES * HEIGHT * WIDTH
VMEM_LIMIT = 56 * 1024 * 1024
BF16, F32 = jnp.bfloat16, jnp.float32

TAPS = [9 * a + 3 * b + e for b in range(3) for a in range(3) for e in range(3)]


def up(value, multiple):
    return -(-value // multiple) * multiple


def params():
    return pltpu.CompilerParams(vmem_limit_bytes=VMEM_LIMIT)


def roll(x, shift):
    size = x.shape[-1]
    shift = shift % size
    return pltpu.roll(x, shift, x.ndim - 1) if shift else x


def exact_dot(x, y):
    return jnp.dot(x, y, preferred_element_type=F32, precision=lax.Precision.HIGHEST)


class Layout:
    def __init__(self, n, clip_ref, rows_ref, cols_ref, start_ref):
        position = lax.axis_index("tile")
        self.n = n
        self.core = lax.rem(position, 2)
        self.chip = lax.div(position, 2)
        self.tiles, self.clip, self.rows, self.cols, self.start = [], [], [], [], []
        self.above, self.below = [], []
        for m in range(n):
            tile = lax.rem(2 * self.chip + m, n)
            clip = clip_ref[0, tile]
            self.clip.append(clip)
            self.rows.append(rows_ref[0, tile])
            self.cols.append(cols_ref[0, clip])
            self.start.append(start_ref[0, clip])
            over = clip_ref[0, jnp.maximum(tile - 1, 0)]
            under = clip_ref[0, jnp.minimum(tile + 1, n - 1)]
            self.above.append(((tile > 0) & (over == clip)).astype(jnp.int32))
            self.below.append(((tile < n - 1) & (under == clip)).astype(jnp.int32))
        cell = lax.broadcasted_iota(jnp.int32, (1, CELLS), 1)
        self.f = lax.shift_right_logical(cell, 6)
        self.r = lax.bitwise_and(lax.shift_right_logical(cell, 3), 7)
        self.c = lax.bitwise_and(cell, 7)

    def valid(self, m):
        inside = (self.f >= self.start[m]) & (self.r < self.rows[m]) & (self.c < self.cols[m])
        return inside.astype(F32)

    def valid_rows(self, m):
        cell = lax.broadcasted_iota(jnp.int32, (CELLS, WIDE), 0)
        f = lax.shift_right_logical(cell, 6)
        r = lax.bitwise_and(lax.shift_right_logical(cell, 3), 7)
        c = lax.bitwise_and(cell, 7)
        return ((f >= self.start[m]) & (r < self.rows[m]) & (c < self.cols[m])).astype(F32)

    def lanes(self, parts):
        return jnp.concatenate(parts, axis=1)

    def repeat(self, part, count=None):
        return jnp.concatenate([part] * (count or self.n), axis=1)

    def counted(self, group_size):
        lane = lax.broadcasted_iota(jnp.int32, (1, 128), 1)
        counted = jnp.ones((1, 128), jnp.int32)
        for m in range(self.n):
            clip_rows = jnp.int32(0)
            for other in range(self.n):
                clip_rows += jnp.where(self.clip[other] == self.clip[m], self.rows[other], 0)
            cells = (FRAMES - self.start[m]) * self.cols[m] * clip_rows * group_size
            counted = jnp.where(lane == m, cells, counted)
        return counted.astype(F32)

    def clip_totals(self, sums):
        lane = lax.broadcasted_iota(jnp.int32, (1, 128), 1)
        total = jnp.zeros((sums[0].shape[0], 128), F32)
        for m in range(self.n):
            same = jnp.zeros((1, 128), F32)
            for other in range(self.n):
                hit = (self.clip[other] == self.clip[m]).astype(F32)
                same = jnp.where(lane == other, hit, same)
            total = total + sums[m] * same
        return total


def group_matrix(rows, real, padded, group_size):
    def group(index):
        block = index // padded
        inner = index - block * padded
        channel = block * real + inner
        return jnp.where(inner < real, channel // group_size, -1 - index)

    first = group(lax.broadcasted_iota(jnp.int32, (rows, rows), 0))
    second = group(lax.broadcasted_iota(jnp.int32, (rows, rows), 1))
    return (first == second).astype(F32)


def column(row_ref, channel_of, rows):
    channels = row_ref.shape[1]
    lane = lax.broadcasted_iota(jnp.int32, (rows, channels), 1)
    index = channel_of(lax.broadcasted_iota(jnp.int32, (rows, channels), 0))
    return jnp.sum(jnp.where(lane == index, row_ref[...], 0.0), axis=1, keepdims=True)


def own_channels(first, real, padded):
    def channel(index):
        block = index // padded
        inner = index - block * padded
        return jnp.where(inner < real, first + block * real + inner, -1)

    return channel


def prepare_kernel(nc, ir, irp, x_ref, g_ref, w_ref, *rest):
    outs, (w_out, blocks, wide, packed) = rest[:nc], rest[nc:]
    cbp = 2 * irp
    chip = lax.div(lax.axis_index("tile"), 2)
    turned = x_ref[...].astype(F32).T
    if irp != ir:
        blocks[...] = jnp.zeros_like(blocks)
    for q in range(nc):
        for core in range(2):
            at = (2 * q + core) * ir
            blocks[q, core * irp : core * irp + ir, :] = turned[at : at + ir]
    low = g_ref[:, :128]
    high = g_ref[:, 128:192].astype(F32)
    high = jnp.concatenate([high[: CELLS // 2], high[CELLS // 2 :]], axis=1).astype(BF16)
    for j in range(nc):
        mine = blocks[lax.rem(chip + j, nc)].astype(BF16)
        out = outs[j]
        out[0:cbp] = mine[:, :128]
        out[cbp : 2 * cbp] = mine[:, 128:]
        out[2 * cbp : 2 * cbp + CELLS] = low
        out[2 * cbp + CELLS :] = high
    ob = w_ref.shape[2]
    wide[...] = w_ref[...].astype(F32)
    packed[...] = jnp.zeros_like(packed)
    for p in range(HALF_TAPS):
        packed[p * irp : p * irp + ir, 0:ob] = wide[:, TAPS[p], :]
        if p + HALF_TAPS < 27:
            packed[p * irp : p * irp + ir, 64 : 64 + ob] = wide[:, TAPS[p + HALF_TAPS], :]
    w_out[...] = packed[...].astype(BF16)


def feature_block(ref, cbp):
    return jnp.concatenate([ref[0:cbp], ref[cbp : 2 * cbp]], axis=1).astype(F32)


def load_weight(refs, ob):
    nd = len(refs)
    dp = lax.axis_index("dp")
    joined = jnp.concatenate([ref[...] for ref in refs], axis=1)
    halves = []
    for start in (0, 64):
        picks = []
        for j in range(nd):
            lane = lax.broadcasted_iota(jnp.int32, (128, WIDE), 0) - start
            out = lax.broadcasted_iota(jnp.int32, (128, WIDE), 1) - lax.rem(dp + j, nd) * ob
            picks.append(((lane == out) & (lane >= 0) & (lane < ob)).astype(F32))
        pick = jnp.concatenate(picks, axis=0).astype(BF16)
        halves.append(jnp.dot(joined, pick, preferred_element_type=F32))
    return jnp.concatenate(halves, axis=0)


def conv_kernel(nc, nd, ir, irp, ob, group_size, *refs):
    n = 2 * nc
    cbp = 2 * irp
    table, refs = refs[:4], refs[4:]
    gamma_ref, beta_ref = refs[:2]
    refs = refs[2:]
    own, other, refs = refs[:nc], refs[nc:n], refs[n:]
    w_own, w_other, refs = refs[:nd], refs[nd : 2 * nd], refs[2 * nd :]
    outs, (stats_out, hidden_out, patches) = refs[:nc], refs[nc:]
    place = Layout(n, *table)
    even = place.core == 0
    channel = own_channels(place.chip * 2 * ir, ir, irp)
    gamma = column(gamma_ref, channel, cbp)
    beta = column(beta_ref, channel, cbp)
    masked, valid, first, square = [], [], [], []
    for k in range(nc):
        mine, theirs = feature_block(own[k], cbp), feature_block(other[k], cbp)
        for p, block in enumerate((jnp.where(even, mine, theirs), jnp.where(even, theirs, mine))):
            keep = place.valid(2 * k + p)
            block = block * keep
            valid.append(keep)
            masked.append(block)
            first.append(jnp.sum(block, axis=1, keepdims=True))
            square.append(jnp.sum(block * block, axis=1, keepdims=True))
    groups = group_matrix(cbp, ir, irp, group_size)
    counted = place.counted(group_size)
    mean = exact_dot(groups, place.clip_totals(first)) / counted
    variance = exact_dot(groups, place.clip_totals(square)) / counted - mean * mean
    inv_std = lax.rsqrt(variance + EPSILON)
    stats_out[0] = mean
    stats_out[1] = inv_std
    hidden = []
    for m in range(n):
        normed = (masked[m] - mean[:, m : m + 1]) * inv_std[:, m : m + 1]
        activation = normed * gamma + beta
        hidden.append(activation * jax.nn.sigmoid(activation) * valid[m])
    hidden = place.lanes(hidden).astype(BF16).astype(F32)
    top, bottom = hidden[:irp], hidden[irp:]
    mine, theirs = jnp.where(even, top, bottom), jnp.where(even, bottom, top)
    hidden_out[...] = mine.astype(BF16)
    hidden = jnp.concatenate([mine, theirs], axis=0)
    above, below = row_neighbours(place, hidden)

    def own_tiles(x):
        parts = []
        for k in range(nc):
            low = x[:, 2 * k * CELLS : (2 * k + 1) * CELLS]
            high = x[:, (2 * k + 1) * CELLS : (2 * k + 2) * CELLS]
            parts.append(jnp.where(even, low, high))
        return jnp.concatenate(parts, axis=1)

    f, c = place.repeat(place.f, nc), place.repeat(place.c, nc)
    for b, rows in enumerate((above, hidden, below)):
        for a, e, block in shifts(own_tiles(rows), f, c):
            u = 9 * b + 3 * a + e
            patches[u * cbp : (u + 1) * cbp] = block.astype(BF16)
    patches[27 * cbp :] = jnp.zeros((cbp, nc * CELLS), BF16)
    mine, theirs = load_weight(w_own, ob), load_weight(w_other, ob)
    pair = jnp.concatenate(
        [mine.reshape(2 * HALF_TAPS, irp, WIDE), theirs.reshape(2 * HALF_TAPS, irp, WIDE)], axis=1
    ).reshape(2 * HALF_TAPS * cbp, WIDE)
    turned = pair.T[:192].astype(BF16)
    total = jnp.dot(turned, patches[...], preferred_element_type=F32)
    for k in range(nc):
        outs[k][...] = total[:, k * CELLS : (k + 1) * CELLS].astype(outs[k].dtype)


def row_neighbours(place, x):
    r = place.repeat(place.r)
    edge_above = place.lanes([((place.r > 0) | (place.above[m] > 0)).astype(F32) for m in range(place.n)])
    edge_below = place.lanes([((place.r < 7) | (place.below[m] > 0)).astype(F32) for m in range(place.n)])
    above = roll(jnp.where(r == 7, roll(x, CELLS - 64), x), 8) * edge_above
    below = roll(jnp.where(r == 0, roll(x, 64 - CELLS), x), -8) * edge_below
    return above, below


def shifts(x, f, c):
    for e in range(3):
        if e == 0:
            moved = jnp.where(c > 0, roll(x, 1), 0.0)
        elif e == 2:
            moved = jnp.where(c < 7, roll(x, -1), 0.0)
        else:
            moved = x
        for a in range(3):
            late = 2 - a
            yield a, e, (jnp.where(f >= late, roll(moved, 64 * late), 0.0) if late else moved)


def grad_kernel(nc, nd, ir, irp, ob, group_size, *refs):
    n = 2 * nc
    cbp = 2 * irp
    table, refs = refs[:4], refs[4:]
    gamma_ref, beta_ref, stats_ref, hidden_ref = refs[:4]
    refs = refs[4:]
    own, other, refs = refs[:nc], refs[nc:n], refs[n:]
    w_own, refs = refs[:nd], refs[nd:]
    outs, refs = refs[:nc], refs[nc:]
    w_outs, (grads, centre, over, under, patches) = refs[:nd], refs[nd:]
    place = Layout(n, *table)
    even = place.core == 0
    width = n * CELLS
    lane = lax.broadcasted_iota(jnp.int32, (CELLS // 2, 128), 1)
    for k in range(nc):
        for mine, ref in ((True, own[k]), (False, other[k])):
            low = ref[2 * cbp : 2 * cbp + CELLS].astype(F32)
            high = ref[2 * cbp + CELLS :].astype(F32)
            right = jnp.concatenate([jnp.where(lane < 64, high, 0.0), jnp.where(lane < 64, roll(high, 64), 0.0)], axis=0)
            core = place.core if mine else 1 - place.core
            grads[2 * k + core] = jnp.concatenate([low, right], axis=1)
    for m in range(n):
        grads[m] = grads[m] * place.valid_rows(m)
    split = (FRAMES, HEIGHT, WIDTH, WIDE)
    for m in range(n):
        here = grads[m]
        rows = here.reshape(split)
        last = grads[(m - 1) % n].reshape(split)[:, 7:] * place.above[m].astype(F32)
        next_ = grads[(m + 1) % n].reshape(split)[:, :1] * place.below[m].astype(F32)
        at = slice(m * CELLS, (m + 1) * CELLS)
        centre[at] = here.astype(BF16)
        over[at] = jnp.concatenate([last, rows[:, :7]], axis=1).reshape(CELLS, WIDE).astype(BF16)
        under[at] = jnp.concatenate([rows[:, 1:], next_], axis=1).reshape(CELLS, WIDE).astype(BF16)
    weight = load_weight(w_own, ob)
    total = jnp.zeros((9 * irp, width), F32)
    for b, block in enumerate((under, centre, over)):
        part = weight[b * 9 * irp : (b + 1) * 9 * irp].astype(BF16)
        total = total + lax.dot_general(part, block[...], (((1,), (1,)), ((), ())), preferred_element_type=F32)
    f, c = place.repeat(place.f), place.repeat(place.c)
    hidden_grad = jnp.zeros((irp, width), F32)
    for e in range(3):
        moved = jnp.zeros((irp, width), F32)
        for a in range(3):
            late = 2 - a
            block = total[(3 * a + e) * irp : (3 * a + e + 1) * irp]
            moved = moved + (jnp.where(f < FRAMES - late, roll(block, -64 * late), 0.0) if late else block)
        if e == 0:
            moved = jnp.where(c < 7, roll(moved, -1), 0.0)
        elif e == 2:
            moved = jnp.where(c > 0, roll(moved, 1), 0.0)
        hidden_grad = hidden_grad + moved
    first_channel = (place.chip * 2 + place.core) * ir
    channel = own_channels(first_channel, ir, irp)
    gamma = column(gamma_ref, channel, irp)
    beta = column(beta_ref, channel, irp)
    mean = jnp.where(even, stats_ref[0, :irp], stats_ref[0, irp:])
    inv_std = jnp.where(even, stats_ref[1, :irp], stats_ref[1, irp:])
    valid, normed, dnormed, first, second = [], [], [], [], []
    for k in range(nc):
        mine, theirs = feature_block(own[k], cbp), feature_block(other[k], cbp)
        mine = jnp.where(even, mine[:irp], mine[irp:])
        theirs = jnp.where(even, theirs[:irp], theirs[irp:])
        for p, block in enumerate((jnp.where(even, mine, theirs), jnp.where(even, theirs, mine))):
            m = 2 * k + p
            keep = place.valid(m)
            norm = (block * keep - mean[:, m : m + 1]) * inv_std[:, m : m + 1]
            activation = norm * gamma + beta
            s = jax.nn.sigmoid(activation)
            grad = hidden_grad[:, m * CELLS : (m + 1) * CELLS]
            grad = grad * keep * s * (1.0 + activation * (1.0 - s)) * gamma
            valid.append(keep)
            normed.append(norm)
            dnormed.append(grad)
            first.append(jnp.sum(grad, axis=1, keepdims=True))
            second.append(jnp.sum(grad * norm, axis=1, keepdims=True))
    groups = group_matrix(irp, ir, irp, group_size)
    counted = place.counted(group_size)
    first_total = exact_dot(groups, place.clip_totals(first)) / counted
    second_total = exact_dot(groups, place.clip_totals(second)) / counted
    for m in range(n):
        grad = dnormed[m] - first_total[:, m : m + 1] - normed[m] * second_total[:, m : m + 1]
        grad = grad * inv_std[:, m : m + 1] * valid[m]
        outs[m // 2][:, (m % 2) * CELLS : (m % 2 + 1) * CELLS] = grad.astype(BF16)
    hidden = hidden_ref[...].astype(F32)
    above, below = row_neighbours(place, hidden)
    blocks = {}
    for b, rows in enumerate((above, hidden, below)):
        for a, e, block in shifts(rows, f, c):
            blocks[9 * b + 3 * a + e] = block
    blocks[27] = jnp.zeros((irp, width), F32)
    for p in range(HALF_TAPS):
        both = jnp.concatenate([blocks[2 * p], blocks[2 * p + 1]], axis=0)
        patches[p * cbp : (p + 1) * cbp] = both.astype(BF16)
    product = jnp.dot(patches[...], centre[...], preferred_element_type=F32)
    dp = lax.axis_index("dp")
    half = HALF_TAPS * irp
    lane = lax.broadcasted_iota(jnp.int32, (half, 128), 1)
    for j in range(nd):
        target = lax.rem(dp + j, nd)
        moved = pltpu.roll(product, lax.rem(WIDE - target * ob, WIDE), 1)[:, :128]
        low = jnp.where(lane < ob, moved[:half], 0.0)
        high = jnp.where(lane < ob, moved[half:], 0.0)
        w_outs[j][...] = (low + roll(high, 64)).astype(w_outs[j].dtype)


def conv_end_kernel(n, *refs):
    table, bias_ref, mine_ref = refs[:4], refs[4], refs[5]
    received, out_ref = refs[6:-1], refs[-1]
    place = Layout(n, *table)
    position = lax.axis_index("tile")
    total = mine_ref[...]
    for ref in received:
        total = total + ref[...].astype(F32)
    clip = table[0][0, position]
    rows, cols, start = table[1][0, position], table[2][0, clip], table[3][0, clip]
    inside = (place.f >= start) & (place.r < rows) & (place.c < cols)
    bias = column(bias_ref, lambda index: index, total.shape[0])
    out_ref[...] = jnp.where(inside, total + bias, 0.0).T.astype(BF16)


def grad_end_kernel(nc, ir, irp, *refs):
    own, other, out_ref, blocks = refs[:nc], refs[nc : 2 * nc], refs[2 * nc], refs[2 * nc + 1]
    position = lax.axis_index("tile")
    core, chip = lax.rem(position, 2), lax.div(position, 2)
    for j in range(nc):
        source = lax.rem(chip + nc - j, nc)
        for mine, ref in ((True, own[j]), (False, other[j])):
            x = ref[...].astype(F32)
            x = jnp.where(core == 0, x[:, :CELLS], x[:, CELLS:])
            blocks[2 * source + (core if mine else 1 - core)] = x
    joined = jnp.concatenate([blocks[q][:ir] for q in range(2 * nc)], axis=0)
    out_ref[...] = joined.T.astype(BF16)


def weight_end_kernel(ir, irp, ob, mine_ref, *refs):
    received, (out_ref, total) = refs[:-2], refs[-2:]
    value = mine_ref[...]
    for ref in received:
        value = value + ref[...].astype(F32)
    total[...] = value
    for u in range(27):
        p, start = (u, 0) if u < HALF_TAPS else (u - HALF_TAPS, 64)
        out_ref[:, TAPS[u], :] = total[p * irp : p * irp + ir, start : start + ob]


def on_device(
    features, out_grad, weight, bias, gamma, beta, tile_clip, tile_rows, clip_cols, clip_start
):
    n, nd = lax.axis_size("tile"), lax.axis_size("dp")
    nc = n // 2
    channels = features.shape[-1]
    group_size = channels // G
    ir, _, ob = weight.shape
    irp = up(ir, 8)
    cbp = 2 * irp
    width = n * CELLS
    smem = pl.BlockSpec(memory_space=pltpu.SMEM)
    vmem = pl.BlockSpec(memory_space=pltpu.VMEM)
    table = (tile_clip, tile_rows, clip_cols, clip_start)

    def shape(dims, dtype=BF16):
        return jax.ShapeDtypeStruct(dims, dtype)

    def call(kernel, args, out, scratch=(), scalars=0):
        return pl.pallas_call(
            kernel,
            out_shape=out,
            in_specs=[smem] * scalars + [vmem] * (len(args) - scalars),
            out_specs=jax.tree.map(lambda _: vmem, out),
            scratch_shapes=list(scratch),
            compiler_params=params(),
        )(*args)

    def along_chips(x, j):
        pairs = [(2 * q + core, 2 * ((q + j) % nc) + core) for q in range(nc) for core in range(2)]
        return lax.ppermute(x, "tile", pairs)

    def swap(x):
        return lax.ppermute(x, "tile", [(i, i ^ 1) for i in range(n)])

    def along_dp(x, j):
        return lax.ppermute(x, "dp", [(i, (i + j) % nd) for i in range(nd)])

    packed_rows = 2 * cbp + CELLS + CELLS // 2
    sent = call(
        functools.partial(prepare_kernel, nc, ir, irp),
        (features.reshape(CELLS, channels), out_grad.reshape(CELLS, channels), weight),
        [shape((packed_rows, 128))] * nc + [shape((HALF_TAPS * irp, 128))],
        [
            pltpu.VMEM((nc, cbp, CELLS), F32),
            pltpu.VMEM(weight.shape, F32),
            pltpu.VMEM((HALF_TAPS * irp, 128), F32),
        ],
    )
    sent, w_block = sent[:nc], sent[nc]
    own = [sent[0]] + [along_chips(sent[nc - j], nc - j) for j in range(1, nc)]
    other = [swap(x) for x in own]
    w_own = [w_block] + [along_dp(w_block, nd - j) for j in range(1, nd)]
    w_other = [swap(x) for x in w_own]
    gamma, beta, bias = gamma[None], beta[None], bias[None]

    first = call(
        functools.partial(conv_kernel, nc, nd, ir, irp, ob, group_size),
        (*table, gamma, beta, *own, *other, *w_own, *w_other),
        [shape((channels, CELLS), F32)]
        + [shape((channels, CELLS))] * (nc - 1)
        + [shape((2, cbp, 128), F32), shape((irp, width))],
        [pltpu.VMEM((2 * HALF_TAPS * cbp, nc * CELLS), BF16)],
        4,
    )
    parts, stats, hidden = first[:nc], first[nc], first[nc + 1]
    received = [along_chips(parts[j], j) for j in range(1, nc)]

    second = call(
        functools.partial(grad_kernel, nc, nd, ir, irp, ob, group_size),
        (*table, gamma, beta, stats, hidden, *own, *other, *w_own),
        [shape((irp, 2 * CELLS))] * nc
        + [shape((HALF_TAPS * irp, 128), F32)]
        + [shape((HALF_TAPS * irp, 128))] * (nd - 1),
        [
            pltpu.VMEM((n, CELLS, WIDE), F32),
            pltpu.VMEM((width, WIDE), BF16),
            pltpu.VMEM((width, WIDE), BF16),
            pltpu.VMEM((width, WIDE), BF16),
            pltpu.VMEM((HALF_TAPS * cbp, width), BF16),
        ],
        4,
    )
    grads, w_parts = second[:nc], second[nc:]
    w_received = [along_dp(w_parts[j], j) for j in range(1, nd)]
    grads = [grads[0]] + [along_chips(grads[j], j) for j in range(1, nc)]
    grads_other = [swap(x) for x in grads]

    conv_out = call(
        functools.partial(conv_end_kernel, n),
        (*table, bias, parts[0], *received),
        shape((CELLS, channels)),
        (),
        4,
    )
    weight_grad = call(
        functools.partial(weight_end_kernel, ir, irp, ob),
        (w_parts[0], *w_received),
        shape(weight.shape, F32),
        [pltpu.VMEM((HALF_TAPS * irp, 128), F32)],
    )
    input_grad = call(
        functools.partial(grad_end_kernel, nc, ir, irp),
        (*grads, *grads_other),
        shape((CELLS, channels)),
        [pltpu.VMEM((n, irp, CELLS), F32)],
    )
    return (
        conv_out.reshape(features.shape),
        input_grad.reshape(features.shape),
        weight_grad,
    )


def solution(mesh):
    in_specs = (
        P("dp", None, "tile", None, None),
        P("dp", None, "tile", None, None),
        P("tile", None, "dp"),
        P(),
        P(),
        P(),
        P("dp", None),
        P("dp", None),
        P("dp", None),
        P("dp", None),
    )
    out_specs = (
        P("dp", None, "tile", None, None),
        P("dp", None, "tile", None, None),
        P("tile", None, "dp"),
    )
    return jax.shard_map(
        on_device, mesh=mesh, in_specs=in_specs, out_specs=out_specs, check_vma=False
    )
```

```python
import functools

import jax
import jax.numpy as jnp
from jax import lax
from jax.experimental import pallas as pl
from jax.experimental.pallas import tpu as pltpu
from jax.sharding import PartitionSpec as P

G = 32
EPSILON = 1e-05
WIDE = 256
HALF_TAPS = 14
FRAMES, HEIGHT, WIDTH = 4, 8, 8
CELLS = FRAMES * HEIGHT * WIDTH
BF16, F32 = jnp.bfloat16, jnp.float32
NT = (((1,), (1,)), ((), ()))

TAPS = [9 * a + 3 * b + e for b in range(3) for a in range(3) for e in range(3)]


def up(value, multiple):
    return -(-value // multiple) * multiple


def roll(x, shift):
    size = x.shape[-1]
    shift = shift % size
    return pltpu.roll(x, shift, x.ndim - 1) if shift else x


def dot(x, y):
    return jnp.dot(x, y, preferred_element_type=F32)


def exact_dot(x, y):
    return jnp.dot(x, y, preferred_element_type=F32, precision=lax.Precision.HIGHEST)


def place():
    position = lax.axis_index("tile")
    core = lax.rem(position, 2)
    return lax.div(position, 2), core, core == 0


def cell_index(shape, axis):
    cell = lax.broadcasted_iota(jnp.int32, shape, axis)
    return (
        lax.shift_right_logical(cell, 6),
        lax.bitwise_and(lax.shift_right_logical(cell, 3), 7),
        lax.bitwise_and(cell, 7),
    )


def column(row_ref, channel_of, rows):
    channels = row_ref.shape[1]
    lane = lax.broadcasted_iota(jnp.int32, (rows, channels), 1)
    index = channel_of(lax.broadcasted_iota(jnp.int32, (rows, channels), 0))
    return jnp.sum(jnp.where(lane == index, row_ref[...], 0.0), axis=1, keepdims=True)


def block_row(index, real, padded):
    block = index // padded
    return block, index - block * padded


def prepare_kernel(nc, ir, irp, x_hbm, g_hbm, w_hbm, *rest):
    outs, (w_out, x_ref, g_ref, w_ref, blocks, packed, sems) = rest[:nc], rest[nc:]
    cbp = 2 * irp
    ob = w_ref.shape[2]
    copies = [
        pltpu.make_async_copy(src, dst, sems.at[i])
        for i, (src, dst) in enumerate(((x_hbm, x_ref), (g_hbm, g_ref), (w_hbm, w_ref)))
    ]
    for copy in copies:
        copy.start()
    chip = place()[0]
    packed[...] = jnp.zeros_like(packed)
    if irp != ir:
        blocks[...] = jnp.zeros_like(blocks)
    copies[0].wait()
    turned = x_ref[...].astype(F32).T
    for q in range(nc):
        for core in range(2):
            at = (2 * q + core) * ir
            blocks[q, core * irp : core * irp + ir, :] = turned[at : at + ir]
    for j in range(nc):
        mine = blocks[lax.bitwise_xor(chip, j)].astype(BF16)
        outs[j][0:cbp] = mine[:, :128]
        outs[j][cbp : 2 * cbp] = mine[:, 128:]
    copies[1].wait()
    low = g_ref[:, :128]
    high = g_ref[:, 128:192].astype(F32)
    high = jnp.concatenate([high[: CELLS // 2], high[CELLS // 2 :]], axis=1).astype(BF16)
    for j in range(nc):
        outs[j][2 * cbp : 2 * cbp + CELLS] = low
        outs[j][2 * cbp + CELLS :] = high
    copies[2].wait()
    for u in range(27):
        p, start = (u, 0) if u < HALF_TAPS else (u - HALF_TAPS, 64)
        packed[p * irp : p * irp + ir, start : start + ob] = w_ref[TAPS[u]].astype(F32)
    w_out[...] = packed[...].astype(BF16)


def setup_kernel(n, nd, ir, irp, ob, channels, *refs):
    clip_ref, rows_ref, cols_ref, start_ref, gamma_ref, beta_ref, bias_ref = refs[:7]
    w_sets, refs = (refs[7 : 7 + nd], refs[7 + nd : 7 + 2 * nd]), refs[7 + 2 * nd :]
    conv_out, grad_out, lanes_out, rows_out, columns_out, tiles_out, end_out, bias_out = refs
    group_size = channels // G
    cbp = 2 * irp
    chip = place()[0]
    position = lax.axis_index("tile")
    clip = [clip_ref[0, m] for m in range(n)]
    rows = [rows_ref[0, m] for m in range(n)]
    cols = [cols_ref[0, clip[m]] for m in range(n)]
    start = [start_ref[0, clip[m]] for m in range(n)]
    same = [[(clip[k] == clip[m]).astype(jnp.int32) for k in range(n)] for m in range(n)]
    above = [same[m][m - 1] if m else jnp.int32(0) for m in range(n)]
    below = [same[m][m + 1] if m < n - 1 else jnp.int32(0) for m in range(n)]

    def valid(m, f, r, c):
        return (f >= start[m]) & (r < rows[m]) & (c < cols[m])

    f, r, c = cell_index((1, CELLS), 1)
    lanes_out[...] = jnp.zeros_like(lanes_out)
    for m in range(n):
        at = slice(m * CELLS, (m + 1) * CELLS)
        lanes_out[0:1, at] = valid(m, f, r, c).astype(F32)
        lanes_out[1:2, at] = ((r > 0) | (above[m] > 0)).astype(F32)
        lanes_out[2:3, at] = ((r < 7) | (below[m] > 0)).astype(F32)
    own_clip = clip_ref[0, position]
    inside = (f >= start_ref[0, own_clip]) & (r < rows_ref[0, position]) & (c < cols_ref[0, own_clip])
    end_out[...] = jnp.broadcast_to(inside.astype(F32), end_out.shape)
    f, r, c = cell_index((CELLS, 128), 0)
    for m in range(n):
        rows_out[m * CELLS : (m + 1) * CELLS] = valid(m, f, r, c).astype(F32)
    lane = lax.broadcasted_iota(jnp.int32, (1, 128), 1)
    count = jnp.ones((1, 128), jnp.int32)
    tiles_out[...] = jnp.zeros_like(tiles_out)
    for m in range(n):
        clip_rows = jnp.int32(0)
        mates = jnp.zeros((1, 128), jnp.int32)
        for k in range(n):
            clip_rows += same[m][k] * rows[k]
            mates = jnp.where(lane == k, same[m][k], mates)
        cells = (FRAMES - start[m]) * cols[m] * clip_rows * group_size
        count = jnp.where(lane == m, cells, count)
        tiles_out[0, m : m + 1] = mates.astype(F32)
        tiles_out[1, m : m + 1] = jnp.full((1, 128), above[m]).astype(F32)
        tiles_out[2, m : m + 1] = jnp.full((1, 128), below[m]).astype(F32)
    tiles_out[3, 0:1] = count.astype(F32)

    def channel(index):
        block, inner = block_row(index, ir, irp)
        return jnp.where(inner < ir, chip * 2 * ir + block * ir + inner, -1)

    columns_out[0] = jnp.broadcast_to(column(gamma_ref, channel, cbp), (cbp, 128))
    columns_out[1] = jnp.broadcast_to(column(beta_ref, channel, cbp), (cbp, 128))
    bias_out[...] = jnp.broadcast_to(column(bias_ref, lambda index: index, channels), (channels, 128))
    dp = lax.axis_index("dp")
    straight_picks, turned_picks = [], []
    for first in (0, 64):
        picks, flipped = [], []
        for j in range(nd):
            base = lax.bitwise_xor(dp, j) * ob
            for dims, axis, into in (((128, WIDE), 1, picks), ((WIDE, 128), 0, flipped)):
                lane = lax.broadcasted_iota(jnp.int32, dims, 1 - axis) - first
                out = lax.broadcasted_iota(jnp.int32, dims, axis) - base
                into.append(((lane == out) & (lane >= 0) & (lane < ob)).astype(F32))
        straight_picks.append(jnp.concatenate(picks, axis=0).astype(BF16))
        turned_picks.append(jnp.concatenate(flipped, axis=1).astype(BF16))
    pad = grad_out.shape[1] - 9 * irp
    for s, w_refs in enumerate(w_sets):
        joined = jnp.concatenate([ref[...] for ref in w_refs], axis=1)
        turned = [lax.dot_general(pick, joined, NT, preferred_element_type=F32) for pick in turned_picks]
        conv_out[s] = jnp.concatenate(turned, axis=1)[:channels].astype(BF16)
        straight = jnp.concatenate([dot(joined, pick) for pick in straight_picks], axis=0)
        grad = jnp.concatenate([straight[b * 9 * irp : (b + 1) * 9 * irp] for b in range(3)], axis=1)
        if pad:
            grad = jnp.concatenate([grad, jnp.zeros((pad, 3 * WIDE), F32)], axis=0)
        grad_out[s] = grad.astype(BF16)


def row_neighbours(x, edges_ref):
    n = x.shape[1] // CELLS
    r = jnp.concatenate([cell_index((1, CELLS), 1)[1]] * n, axis=1)
    above = roll(jnp.where(r == 7, roll(x, CELLS - 64), x), 8) * edges_ref[1:2, :]
    below = roll(jnp.where(r == 0, roll(x, 64 - CELLS), x), -8) * edges_ref[2:3, :]
    return above, below


def shifts(x, f, c):
    for e in range(3):
        if e == 0:
            moved = jnp.where(c > 0, roll(x, 1), 0.0)
        elif e == 2:
            moved = jnp.where(c < 7, roll(x, -1), 0.0)
        else:
            moved = x
        for a in range(3):
            late = 2 - a
            yield a, e, (jnp.where(f >= late, roll(moved, 64 * late), 0.0) if late else moved)


def store_patches(ref, variants, f, c, irp):
    blocks = {}
    for b, rows in enumerate(variants):
        for a, e, block in shifts(rows, f, c):
            blocks[9 * b + 3 * a + e] = block
    blocks[27] = jnp.zeros_like(blocks[0])
    for p in range(HALF_TAPS):
        both = jnp.concatenate([blocks[2 * p], blocks[2 * p + 1]], axis=0)
        ref[2 * p * irp : 2 * (p + 1) * irp] = both.astype(BF16)


def main_kernel(nc, nd, ir, irp, ob, channels, *refs):
    n = 2 * nc
    cbp = 2 * irp
    width = n * CELLS
    group_size = channels // G
    lanes_ref, rows_ref, columns_ref, tiles_ref = refs[:4]
    conv_weight, grad_weight, refs = *refs[4:6], refs[6:]
    own, other, refs = refs[:nc], refs[nc:n], refs[n:]
    outs, refs = refs[:nc], refs[nc:]
    w_outs, (features, grads, shifted, patches, own_patches, ends) = refs[:nd], refs[nd:]
    chip, core, even = place()
    lane = lax.broadcasted_iota(jnp.int32, (CELLS // 2, 128), 1)
    for j in range(nc):
        source = 2 * lax.bitwise_xor(chip, j)
        for m, ref in ((source + core, own[j]), (source + 1 - core, other[j])):
            features[m] = jnp.concatenate([ref[0:cbp], ref[cbp : 2 * cbp]], axis=1).astype(F32)
            low = ref[2 * cbp : 2 * cbp + CELLS].astype(F32)
            high = ref[2 * cbp + CELLS :].astype(F32)
            right = [jnp.where(lane < 64, high, 0.0), jnp.where(lane < 64, roll(high, 64), 0.0)]
            grads[m] = jnp.concatenate([low, jnp.concatenate(right, axis=0)], axis=1)
    gamma, beta = columns_ref[0][:, :1], columns_ref[1][:, :1]
    counted = tiles_ref[3, 0:1]

    def clip_totals(sums):
        total = jnp.zeros((cbp, 128), F32)
        for m in range(n):
            total = total + sums[m] * tiles_ref[0, m : m + 1]
        return total

    def group_of(axis):
        index = lax.broadcasted_iota(jnp.int32, (cbp, cbp), axis)
        block, inner = block_row(index, ir, irp)
        return jnp.where(inner < ir, (block * ir + inner) // group_size, -1 - index)

    groups = (group_of(0) == group_of(1)).astype(F32)
    valid, first, square = [], [], []
    for m in range(n):
        keep = lanes_ref[0:1, m * CELLS : (m + 1) * CELLS]
        block = features[m] * keep
        features[m] = block
        valid.append(keep)
        first.append(jnp.sum(block, axis=1, keepdims=True))
        square.append(jnp.sum(block * block, axis=1, keepdims=True))
    mean = exact_dot(groups, clip_totals(first)) / counted
    variance = exact_dot(groups, clip_totals(square)) / counted - mean * mean
    inv_std = lax.rsqrt(variance + EPSILON)

    def normed_of(m):
        return (features[m] - mean[:, m : m + 1]) * inv_std[:, m : m + 1]

    hidden = []
    for m in range(n):
        activation = normed_of(m) * gamma + beta
        hidden.append(activation * jax.nn.sigmoid(activation) * valid[m])
    hidden = jnp.concatenate(hidden, axis=1).astype(BF16).astype(F32)
    above, below = row_neighbours(hidden, lanes_ref)

    def own_rows(x):
        return jnp.where(even, x[:irp], x[irp:])

    def other_rows(x):
        return jnp.where(even, x[irp:], x[:irp])

    def own_tiles(x):
        parts = []
        for k in range(nc):
            low = x[:, 2 * k * CELLS : (2 * k + 1) * CELLS]
            high = x[:, (2 * k + 1) * CELLS : (2 * k + 2) * CELLS]
            parts.append(jnp.where(even, low, high))
        return jnp.concatenate(parts, axis=1)

    frame, _, col = cell_index((1, CELLS), 1)
    f, c = jnp.concatenate([frame] * nc, axis=1), jnp.concatenate([col] * nc, axis=1)
    total = None
    for s, rows_of in enumerate((own_rows, other_rows)):
        part = patches.at[s]
        store_patches(part, [own_tiles(rows_of(x)) for x in (above, hidden, below)], f, c, irp)
        product = dot(conv_weight[s], part[...])
        total = product if total is None else total + product
    for k in range(nc):
        ends[k, :channels] = total[:, k * CELLS : (k + 1) * CELLS]

    for m in range(n):
        keep = rows_ref[m * CELLS : (m + 1) * CELLS]
        grads[m] = grads[m] * jnp.concatenate([keep, keep], axis=1)
    split = (FRAMES, HEIGHT, WIDTH, WIDE)
    for m in range(n):
        here = grads[m]
        rows = here.reshape(split)
        has = [jnp.concatenate([tiles_ref[i, m : m + 1]] * 2, axis=1) for i in (1, 2)]
        last = grads[max(m - 1, 0)].reshape(split)[:, 7:] * has[0]
        next_ = grads[min(m + 1, n - 1)].reshape(split)[:, :1] * has[1]
        at = slice(m * CELLS, (m + 1) * CELLS)
        shifted[at, :WIDE] = jnp.concatenate([rows[:, 1:], next_], axis=1).reshape(CELLS, WIDE).astype(BF16)
        shifted[at, WIDE : 2 * WIDE] = here.astype(BF16)
        shifted[at, 2 * WIDE :] = jnp.concatenate([last, rows[:, :7]], axis=1).reshape(CELLS, WIDE).astype(BF16)
    weight = jnp.concatenate([grad_weight[0], grad_weight[1]], axis=0)
    total = lax.dot_general(weight, shifted[...], NT, preferred_element_type=F32)
    f, c = jnp.concatenate([frame] * n, axis=1), jnp.concatenate([col] * n, axis=1)
    halves = []
    for s in range(2):
        base = s * grad_weight.shape[1]
        hidden_grad = jnp.zeros((irp, width), F32)
        for e in range(3):
            moved = jnp.zeros((irp, width), F32)
            for a in range(3):
                late = 2 - a
                at = base + (3 * a + e) * irp
                block = total[at : at + irp]
                moved = moved + (jnp.where(f < FRAMES - late, roll(block, -64 * late), 0.0) if late else block)
            if e == 0:
                moved = jnp.where(c < 7, roll(moved, -1), 0.0)
            elif e == 2:
                moved = jnp.where(c > 0, roll(moved, 1), 0.0)
            hidden_grad = hidden_grad + moved
        halves.append(hidden_grad)
    hidden_grad = jnp.concatenate([jnp.where(even, *halves), jnp.where(even, *halves[::-1])], axis=0)
    dnormed, first, second = [], [], []
    for m in range(n):
        norm = normed_of(m)
        activation = norm * gamma + beta
        s = jax.nn.sigmoid(activation)
        grad = hidden_grad[:, m * CELLS : (m + 1) * CELLS]
        grad = grad * valid[m] * s * (1.0 + activation * (1.0 - s)) * gamma
        dnormed.append(grad)
        first.append(jnp.sum(grad, axis=1, keepdims=True))
        second.append(jnp.sum(grad * norm, axis=1, keepdims=True))
    first_total = exact_dot(groups, clip_totals(first)) / counted
    second_total = exact_dot(groups, clip_totals(second)) / counted
    for k in range(nc):
        pair = []
        for m in (2 * k, 2 * k + 1):
            grad = dnormed[m] - first_total[:, m : m + 1] - normed_of(m) * second_total[:, m : m + 1]
            pair.append(grad * inv_std[:, m : m + 1] * valid[m])
        ends[k, channels:] = jnp.where(even, *pair)
    for j in range(nc):
        outs[j][...] = ends[lax.bitwise_xor(chip, j)].astype(outs[j].dtype)

    store_patches(own_patches, [own_rows(x) for x in (above, hidden, below)], f, c, irp)
    product = dot(own_patches[...], shifted[:, WIDE : 2 * WIDE])
    dp = lax.axis_index("dp")
    half = HALF_TAPS * irp
    lane = lax.broadcasted_iota(jnp.int32, (half, 128), 1)
    for j in range(nd):
        target = lax.bitwise_xor(dp, j)
        moved = pltpu.roll(product, lax.rem(WIDE - target * ob, WIDE), 1)[:, :128]
        low = jnp.where(lane < ob, moved[:half], 0.0)
        high = jnp.where(lane < ob, moved[half:], 0.0)
        w_outs[j][...] = (low + roll(high, 64)).astype(w_outs[j].dtype)


def end_kernel(n, nd, ir, irp, ob, channels, *refs):
    nc = n // 2
    bias_ref, inside_ref, refs = refs[0], refs[1], refs[2:]
    received, refs = refs[:nc], refs[nc:]
    w_refs, refs = refs[:nd], refs[nd:]
    conv_ref, grad_ref, weight_ref, blocks, total = refs
    chip = place()[0]
    value = w_refs[0][...]
    for ref in w_refs[1:]:
        value = value + ref[...].astype(F32)
    total[...] = value
    for u in range(27):
        p, at = (u, 0) if u < HALF_TAPS else (u - HALF_TAPS, 64)
        weight_ref[TAPS[u]] = total[p * irp : p * irp + ir, at : at + ob]
    conv = received[0][:channels]
    for ref in received[1:]:
        conv = conv + ref[:channels].astype(F32)
    bias = bias_ref[...]
    conv = (conv + jnp.concatenate([bias, bias], axis=1)) * inside_ref[0:1]
    conv_ref[...] = conv.T.astype(BF16)
    for j in range(nc):
        blocks[lax.bitwise_xor(chip, j)] = received[j][channels:].astype(F32)
    parts = [blocks[q, core * irp : core * irp + ir] for q in range(nc) for core in range(2)]
    grad_ref[...] = jnp.concatenate(parts, axis=0).T.astype(BF16)


def on_device(
    features, out_grad, weight, bias, gamma, beta, tile_clip, tile_rows, clip_cols, clip_start
):
    n, nd = lax.axis_size("tile"), lax.axis_size("dp")
    nc = n // 2
    channels = features.shape[-1]
    ir, _, ob = weight.shape
    irp = up(ir, 8)
    cbp = 2 * irp
    width = n * CELLS
    half = HALF_TAPS * irp
    smem = pl.BlockSpec(memory_space=pltpu.SMEM)
    vmem = pl.BlockSpec(memory_space=pltpu.VMEM)
    hbm = pl.BlockSpec(memory_space=pltpu.HBM)

    def shape(dims, dtype=BF16):
        return jax.ShapeDtypeStruct(dims, dtype)

    def call(kernel, args, out, scratch=(), specs=None, us=1.0, room=8, after=()):
        def body(*refs):
            kernel[0](*kernel[1:], *refs[: len(args)], *refs[len(args) + len(after) :])

        return pl.pallas_call(
            body,
            out_shape=out,
            in_specs=(specs or [vmem] * len(args)) + [hbm] * len(after),
            out_specs=jax.tree.map(lambda _: vmem, out),
            scratch_shapes=list(scratch),
            compiler_params=pltpu.CompilerParams(vmem_limit_bytes=room << 20),
            cost_estimate=pl.CostEstimate(flops=int(us * 1e9), bytes_accessed=0, transcendentals=0),
        )(*args, *after)

    def along_chips(x, j):
        return lax.ppermute(x, "tile", [(i, i ^ (2 * j)) for i in range(n)])

    def swap(x):
        return lax.ppermute(x, "tile", [(i, i ^ 1) for i in range(n)])

    def along_dp(x, j):
        return lax.ppermute(x, "dp", [(i, i ^ j) for i in range(nd)])

    packed_rows = 2 * cbp + CELLS + CELLS // 2
    sent = call(
        (prepare_kernel, nc, ir, irp),
        tuple(
            pltpu.with_memory_space_constraint(x, pltpu.HBM)
            for x in (
                features.reshape(CELLS, channels),
                out_grad.reshape(CELLS, channels),
                weight.transpose(1, 0, 2),
            )
        ),
        [shape((packed_rows, 128))] * nc + [shape((half, 128))],
        [
            pltpu.VMEM((CELLS, channels), BF16),
            pltpu.VMEM((CELLS, channels), BF16),
            pltpu.VMEM((27, ir, ob), BF16),
            pltpu.VMEM((nc, cbp, CELLS), F32),
            pltpu.VMEM((half, 128), F32),
            pltpu.SemaphoreType.DMA((3,)),
        ],
        [hbm] * 3,
    )
    sent, w_block = sent[:nc], sent[nc]
    own = [sent[0]] + [along_chips(sent[j], j) for j in range(1, nc)]
    other = [swap(x) for x in own]
    w_blocks = [w_block] + [along_dp(w_block, j) for j in range(1, nd)]
    w_blocks += [swap(x) for x in w_blocks]

    tables = (tile_clip, tile_rows, clip_cols, clip_start)
    ready = call(
        (setup_kernel, n, nd, ir, irp, ob, channels),
        (*tables, gamma[None], beta[None], bias[None], *w_blocks),
        [
            shape((2, channels, 2 * half)),
            shape((2, up(9 * irp, 16), 3 * WIDE)),
            shape((8, width), F32),
            shape((width, 128), F32),
            shape((2, cbp, 128), F32),
            shape((4, up(n, 8), 128), F32),
            shape((8, CELLS), F32),
            shape((channels, 128), F32),
        ],
        (),
        [smem] * 4 + [vmem] * (3 + 2 * nd),
        after=own[-1:],
    )
    conv_weight, grad_weight, lanes, rows, columns, tiles, inside, bias_columns = ready

    parts = call(
        (main_kernel, nc, nd, ir, irp, ob, channels),
        (lanes, rows, columns, tiles, conv_weight, grad_weight)
        + (*own, *other),
        [shape((channels + cbp, CELLS), F32)]
        + [shape((channels + cbp, CELLS))] * (nc - 1)
        + [shape((half, 128), F32)]
        + [shape((half, 128))] * (nd - 1),
        [
            pltpu.VMEM((n, cbp, CELLS), F32),
            pltpu.VMEM((n, CELLS, WIDE), F32),
            pltpu.VMEM((width, 3 * WIDE), BF16),
            pltpu.VMEM((2, 2 * half, nc * CELLS), BF16),
            pltpu.VMEM((2 * half, width), BF16),
            pltpu.VMEM((nc, channels + cbp, CELLS), F32),
        ],
        None,
        8.0,
        16 + 5 * n // 4,
    )
    ends, w_parts = parts[:nc], parts[nc:]
    w_received = [w_parts[0]] + [along_dp(w_parts[j], j) for j in range(1, nd)]
    ends = [ends[0]] + [along_chips(ends[j], j) for j in range(1, nc)]
    conv_out, input_grad, weight_grad = call(
        (end_kernel, n, nd, ir, irp, ob, channels),
        (bias_columns, inside, *ends, *w_received),
        [shape((CELLS, channels)), shape((CELLS, channels)), shape((27, ir, ob), F32)],
        [pltpu.VMEM((nc, cbp, CELLS), F32), pltpu.VMEM((half, 128), F32)],
    )
    return (
        conv_out.reshape(features.shape),
        input_grad.reshape(features.shape),
        weight_grad.transpose(1, 0, 2),
    )


def solution(mesh):
    in_specs = (
        P("dp", None, "tile", None, None),
        P("dp", None, "tile", None, None),
        P("tile", None, "dp"),
        P(),
        P(),
        P(),
        P("dp", None),
        P("dp", None),
        P("dp", None),
        P("dp", None),
    )
    out_specs = (
        P("dp", None, "tile", None, None),
        P("dp", None, "tile", None, None),
        P("tile", None, "dp"),
    )
    return jax.shard_map(
        on_device, mesh=mesh, in_specs=in_specs, out_specs=out_specs, check_vma=False
    )
```

```python
import functools

import jax
import jax.numpy as jnp
from jax import lax
from jax.experimental import pallas as pl
from jax.experimental.pallas import tpu as pltpu
from jax.sharding import PartitionSpec as P

G = 32
EPSILON = 1e-05
WIDE = 256
HALF_TAPS = 14
FRAMES, HEIGHT, WIDTH = 4, 8, 8
CELLS = FRAMES * HEIGHT * WIDTH
BF16, F32 = jnp.bfloat16, jnp.float32
NT = (((1,), (1,)), ((), ()))

def up(value, multiple):
    return -(-value // multiple) * multiple


def roll(x, shift):
    size = x.shape[-1]
    shift = shift % size
    return pltpu.roll(x, shift, x.ndim - 1) if shift else x


def dot(x, y):
    return jnp.dot(x, y, preferred_element_type=F32)


def exact_dot(x, y):
    return jnp.dot(x, y, preferred_element_type=F32, precision=lax.Precision.HIGHEST)


def place():
    position = lax.axis_index("tile")
    core = lax.rem(position, 2)
    return lax.div(position, 2), core, core == 0


def cell_index(shape, axis):
    cell = lax.broadcasted_iota(jnp.int32, shape, axis)
    return (
        lax.shift_right_logical(cell, 6),
        lax.bitwise_and(lax.shift_right_logical(cell, 3), 7),
        lax.bitwise_and(cell, 7),
    )


def column(row_ref, channel_of, rows):
    channels = row_ref.shape[1]
    lane = lax.broadcasted_iota(jnp.int32, (rows, channels), 1)
    index = channel_of(lax.broadcasted_iota(jnp.int32, (rows, channels), 0))
    return jnp.sum(jnp.where(lane == index, row_ref[...], 0.0), axis=1, keepdims=True)


def block_row(index, real, padded):
    block = index // padded
    return block, index - block * padded


def prepare_kernel(nc, ir, irp, x_hbm, g_hbm, w_hbm, *rest):
    outs, (w_ref, x_ref, g_ref, blocks, sems) = rest[:nc], rest[nc:]
    cbp = 2 * irp
    copies = [
        pltpu.make_async_copy(src, dst, sems.at[i])
        for i, (src, dst) in enumerate(((x_hbm, x_ref), (g_hbm, g_ref), (w_hbm, w_ref)))
    ]
    for copy in copies:
        copy.start()
    chip = place()[0]
    if irp != ir:
        blocks[...] = jnp.zeros_like(blocks)
    copies[0].wait()
    turned = x_ref[...].astype(F32).T
    for q in range(nc):
        for core in range(2):
            at = (2 * q + core) * ir
            blocks[q, core * irp : core * irp + ir, :] = turned[at : at + ir]
    for j in range(nc):
        mine = blocks[lax.bitwise_xor(chip, j)].astype(BF16)
        outs[j][0:cbp] = mine[:, :128]
        outs[j][cbp : 2 * cbp] = mine[:, 128:]
    copies[1].wait()
    low = g_ref[:, :128]
    high = g_ref[:, 128:192].astype(F32)
    high = jnp.concatenate([high[: CELLS // 2], high[CELLS // 2 :]], axis=1).astype(BF16)
    for j in range(nc):
        outs[j][2 * cbp : 2 * cbp + CELLS] = low
        outs[j][2 * cbp + CELLS :] = high
    copies[2].wait()


def pack_kernel(ir, irp, ob, own_ref, other_ref, out_ref, packed):
    cbp = 2 * irp
    even = place()[2]
    packed[...] = jnp.zeros_like(packed)
    for u in range(27):
        p, start = (u, 0) if u < HALF_TAPS else (u - HALF_TAPS, 64)
        mine, theirs = own_ref[u].astype(F32), other_ref[u].astype(F32)
        at = p * cbp
        packed[at : at + ir, start : start + ob] = jnp.where(even, mine, theirs)
        packed[at + irp : at + irp + ir, start : start + ob] = jnp.where(even, theirs, mine)
    out_ref[...] = packed[...].astype(BF16)


def tables_kernel(n, nd, ir, irp, ob, channels, *refs):
    clip_ref, rows_ref, cols_ref, start_ref, gamma_ref, beta_ref, bias_ref = refs[:7]
    lanes_out, rows_out, columns_out, tiles_out, end_out, bias_out, pick_out, turned_out = refs[7:]
    group_size = channels // G
    cbp = 2 * irp
    chip = place()[0]
    position = lax.axis_index("tile")
    clip = [clip_ref[0, m] for m in range(n)]
    rows = [rows_ref[0, m] for m in range(n)]
    cols = [cols_ref[0, clip[m]] for m in range(n)]
    start = [start_ref[0, clip[m]] for m in range(n)]
    same = [[(clip[k] == clip[m]).astype(jnp.int32) for k in range(n)] for m in range(n)]
    above = [same[m][m - 1] if m else jnp.int32(0) for m in range(n)]
    below = [same[m][m + 1] if m < n - 1 else jnp.int32(0) for m in range(n)]

    def valid(m, f, r, c):
        return (f >= start[m]) & (r < rows[m]) & (c < cols[m])

    f, r, c = cell_index((1, CELLS), 1)
    lanes_out[...] = jnp.zeros_like(lanes_out)
    for m in range(n):
        at = slice(m * CELLS, (m + 1) * CELLS)
        lanes_out[0:1, at] = valid(m, f, r, c).astype(F32)
        lanes_out[1:2, at] = ((r > 0) | (above[m] > 0)).astype(F32)
        lanes_out[2:3, at] = ((r < 7) | (below[m] > 0)).astype(F32)
    own_clip = clip_ref[0, position]
    inside = (f >= start_ref[0, own_clip]) & (r < rows_ref[0, position]) & (c < cols_ref[0, own_clip])
    end_out[...] = jnp.broadcast_to(inside.astype(F32), end_out.shape)
    f, r, c = cell_index((CELLS, 128), 0)
    for m in range(n):
        rows_out[m * CELLS : (m + 1) * CELLS] = valid(m, f, r, c).astype(F32)
    lane = lax.broadcasted_iota(jnp.int32, (1, 128), 1)
    count = jnp.ones((1, 128), jnp.int32)
    tiles_out[...] = jnp.zeros_like(tiles_out)
    for m in range(n):
        clip_rows = jnp.int32(0)
        mates = jnp.zeros((1, 128), jnp.int32)
        for k in range(n):
            clip_rows += same[m][k] * rows[k]
            mates = jnp.where(lane == k, same[m][k], mates)
        cells = (FRAMES - start[m]) * cols[m] * clip_rows * group_size
        count = jnp.where(lane == m, cells, count)
        tiles_out[0, m : m + 1] = mates.astype(F32)
        tiles_out[1, m : m + 1] = jnp.full((1, 128), above[m]).astype(F32)
        tiles_out[2, m : m + 1] = jnp.full((1, 128), below[m]).astype(F32)
    tiles_out[3, 0:1] = count.astype(F32)

    def channel(index):
        block, inner = block_row(index, ir, irp)
        return jnp.where(inner < ir, chip * 2 * ir + block * ir + inner, -1)

    columns_out[0] = jnp.broadcast_to(column(gamma_ref, channel, cbp), (cbp, 128))
    columns_out[1] = jnp.broadcast_to(column(beta_ref, channel, cbp), (cbp, 128))
    bias_out[...] = jnp.broadcast_to(column(bias_ref, lambda index: index, channels), (channels, 128))
    dp = lax.axis_index("dp")
    for half, first in enumerate((0, 64)):
        for j in range(nd):
            base = lax.bitwise_xor(dp, j) * ob
            at = slice(j * 128, (j + 1) * 128)
            for dims, axis in (((128, WIDE), 1), ((WIDE, 128), 0)):
                lane = lax.broadcasted_iota(jnp.int32, dims, 1 - axis) - first
                out = lax.broadcasted_iota(jnp.int32, dims, axis) - base
                pick = ((lane == out) & (lane >= 0) & (lane < ob)).astype(F32).astype(BF16)
                if axis:
                    pick_out[half, at] = pick
                else:
                    turned_out[half, :, at] = pick


def weight_kernel(nd, ir, irp, channels, pick_ref, turned_ref, *refs):
    conv_out, grad_out = refs[nd:]
    cbp = 2 * irp
    joined = jnp.concatenate([ref[...] for ref in refs[:nd]], axis=1)
    low, high = (lax.dot_general(turned_ref[i], joined, NT, preferred_element_type=F32)[:channels] for i in range(2))
    frames = (
        low[:, : 9 * cbp],
        jnp.concatenate([low[:, 9 * cbp :], high[:, : 4 * cbp]], axis=1),
        high[:, 4 * cbp : 13 * cbp],
    )
    for a in range(3):
        conv_out[a] = frames[a].astype(BF16)
    straight = jnp.concatenate([dot(joined, pick_ref[i]) for i in range(2)], axis=0)
    for b in range(3):
        taps = [9 * a + 3 * b + e for a in range(3) for e in range(3)]
        part = jnp.concatenate([straight[t * cbp : (t + 1) * cbp] for t in taps], axis=0)
        grad_out[:, b * WIDE : (b + 1) * WIDE] = part.astype(BF16)


def row_neighbours(x, edges_ref):
    n = x.shape[1] // CELLS
    r = jnp.concatenate([cell_index((1, CELLS), 1)[1]] * n, axis=1)
    above = roll(jnp.where(r == 7, roll(x, CELLS - 64), x), 8) * edges_ref[1:2, :]
    below = roll(jnp.where(r == 0, roll(x, 64 - CELLS), x), -8) * edges_ref[2:3, :]
    return above, below


def columns(x, c):
    return jnp.where(c > 0, roll(x, 1), 0.0), x, jnp.where(c < 7, roll(x, -1), 0.0)


def later(x, f, late):
    return jnp.where(f >= late, roll(x, 64 * late), 0.0) if late else x


def main_kernel(nc, nd, ir, irp, ob, channels, *refs):
    n = 2 * nc
    cbp = 2 * irp
    width = n * CELLS
    group_size = channels // G
    lanes_ref, rows_ref, columns_ref, tiles_ref = refs[:4]
    conv_weight, grad_weight, refs = *refs[4:6], refs[6:]
    own, other, refs = refs[:nc], refs[nc:n], refs[n:]
    outs, refs = refs[:nc], refs[nc:]
    centre, hidden_out, features, grads, under, over, patches, ends = refs
    chip, core, even = place()
    lane = lax.broadcasted_iota(jnp.int32, (CELLS // 2, 128), 1)
    for j in range(nc):
        source = 2 * lax.bitwise_xor(chip, j)
        for m, ref in ((source + core, own[j]), (source + 1 - core, other[j])):
            features[m] = jnp.concatenate([ref[0:cbp], ref[cbp : 2 * cbp]], axis=1).astype(F32)
            low = ref[2 * cbp : 2 * cbp + CELLS].astype(F32)
            high = ref[2 * cbp + CELLS :].astype(F32)
            right = [jnp.where(lane < 64, high, 0.0), jnp.where(lane < 64, roll(high, 64), 0.0)]
            grads[m] = jnp.concatenate([low, jnp.concatenate(right, axis=0)], axis=1)
    gamma, beta = columns_ref[0][:, :1], columns_ref[1][:, :1]
    counted = tiles_ref[3, 0:1]

    def clip_totals(sums):
        total = jnp.zeros((cbp, 128), F32)
        for m in range(n):
            total = total + sums[m] * tiles_ref[0, m : m + 1]
        return total

    def group_of(axis):
        index = lax.broadcasted_iota(jnp.int32, (cbp, cbp), axis)
        block, inner = block_row(index, ir, irp)
        return jnp.where(inner < ir, (block * ir + inner) // group_size, -1 - index)

    groups = (group_of(0) == group_of(1)).astype(F32)
    valid, first, square = [], [], []
    for m in range(n):
        keep = lanes_ref[0:1, m * CELLS : (m + 1) * CELLS]
        block = features[m] * keep
        features[m] = block
        valid.append(keep)
        first.append(jnp.sum(block, axis=1, keepdims=True))
        square.append(jnp.sum(block * block, axis=1, keepdims=True))
    mean = exact_dot(groups, clip_totals(first)) / counted
    variance = exact_dot(groups, clip_totals(square)) / counted - mean * mean
    inv_std = lax.rsqrt(variance + EPSILON)

    def normed_of(m):
        return (features[m] - mean[:, m : m + 1]) * inv_std[:, m : m + 1]

    hidden = []
    for m in range(n):
        activation = normed_of(m) * gamma + beta
        hidden.append(activation * jax.nn.sigmoid(activation) * valid[m])
    hidden = jnp.concatenate(hidden, axis=1).astype(BF16).astype(F32)
    above, below = row_neighbours(hidden, lanes_ref)

    for b, x in enumerate((above, hidden, below)):
        hidden_out[b] = jnp.where(even, x[:irp], x[irp:]).astype(BF16)

    def own_tiles(x):
        parts = []
        for k in range(nc):
            low = x[:, 2 * k * CELLS : (2 * k + 1) * CELLS]
            high = x[:, (2 * k + 1) * CELLS : (2 * k + 2) * CELLS]
            parts.append(jnp.where(even, low, high))
        return jnp.concatenate(parts, axis=1)

    frame, _, col = cell_index((1, CELLS), 1)
    f, c = jnp.concatenate([frame] * nc, axis=1), jnp.concatenate([col] * nc, axis=1)
    for b, x in enumerate((above, hidden, below)):
        for e, block in enumerate(columns(own_tiles(x), c)):
            at = (3 * b + e) * cbp
            patches[at : at + cbp] = block.astype(BF16)
    total = jnp.zeros((channels, nc * CELLS), F32)
    for a in range(3):
        total = total + later(dot(conv_weight[a], patches[...]), f, 2 - a)
    for k in range(nc):
        ends[k, :channels] = total[:, k * CELLS : (k + 1) * CELLS]

    for m in range(n):
        keep = rows_ref[m * CELLS : (m + 1) * CELLS]
        grads[m] = grads[m] * jnp.concatenate([keep, keep], axis=1)
    split = (FRAMES, HEIGHT, WIDTH, WIDE)
    for m in range(n):
        here = grads[m]
        rows = here.reshape(split)
        has = [jnp.concatenate([tiles_ref[i, m : m + 1]] * 2, axis=1) for i in (1, 2)]
        last = grads[max(m - 1, 0)].reshape(split)[:, 7:] * has[0]
        next_ = grads[min(m + 1, n - 1)].reshape(split)[:, :1] * has[1]
        at = slice(m * CELLS, (m + 1) * CELLS)
        under[at] = jnp.concatenate([rows[:, 1:], next_], axis=1).reshape(CELLS, WIDE).astype(BF16)
        centre[at] = here.astype(BF16)
        over[at] = jnp.concatenate([last, rows[:, :7]], axis=1).reshape(CELLS, WIDE).astype(BF16)
    rows = jnp.concatenate([under[...], centre[...], over[...]], axis=1)
    total = lax.dot_general(grad_weight[...], rows, NT, preferred_element_type=F32)
    f, c = jnp.concatenate([frame] * n, axis=1), jnp.concatenate([col] * n, axis=1)
    hidden_grad = jnp.zeros((cbp, width), F32)
    for e in range(3):
        moved = jnp.zeros((cbp, width), F32)
        for a in range(3):
            late = 2 - a
            block = total[(3 * a + e) * cbp : (3 * a + e + 1) * cbp]
            moved = moved + (jnp.where(f < FRAMES - late, roll(block, -64 * late), 0.0) if late else block)
        if e == 0:
            moved = jnp.where(c < 7, roll(moved, -1), 0.0)
        elif e == 2:
            moved = jnp.where(c > 0, roll(moved, 1), 0.0)
        hidden_grad = hidden_grad + moved
    dnormed, first, second = [], [], []
    for m in range(n):
        norm = normed_of(m)
        activation = norm * gamma + beta
        s = jax.nn.sigmoid(activation)
        grad = hidden_grad[:, m * CELLS : (m + 1) * CELLS]
        grad = grad * valid[m] * s * (1.0 + activation * (1.0 - s)) * gamma
        dnormed.append(grad)
        first.append(jnp.sum(grad, axis=1, keepdims=True))
        second.append(jnp.sum(grad * norm, axis=1, keepdims=True))
    first_total = exact_dot(groups, clip_totals(first)) / counted
    second_total = exact_dot(groups, clip_totals(second)) / counted
    for k in range(nc):
        pair = []
        for m in (2 * k, 2 * k + 1):
            grad = dnormed[m] - first_total[:, m : m + 1] - normed_of(m) * second_total[:, m : m + 1]
            pair.append(grad * inv_std[:, m : m + 1] * valid[m])
        ends[k, channels:] = jnp.where(even, *pair)
    for j in range(nc):
        outs[j][...] = ends[lax.bitwise_xor(chip, j)].astype(outs[j].dtype)


def weight_grad_kernel(n, nd, irp, ob, hidden_ref, centre_ref, *refs):
    w_outs, patches = refs[:nd], refs[nd]
    cbp = 2 * irp
    frame, _, col = cell_index((1, CELLS), 1)
    f, c = jnp.concatenate([frame] * n, axis=1), jnp.concatenate([col] * n, axis=1)
    blocks = {}
    for b in range(3):
        for e, block in enumerate(columns(hidden_ref[b].astype(F32), c)):
            for a in range(3):
                blocks[9 * a + 3 * b + e] = later(block, f, 2 - a)
    blocks[27] = jnp.zeros_like(blocks[0])
    for p in range(HALF_TAPS):
        both = jnp.concatenate([blocks[2 * p], blocks[2 * p + 1]], axis=0)
        patches[p * cbp : (p + 1) * cbp] = both.astype(BF16)
    product = dot(patches[...], centre_ref[...])
    dp = lax.axis_index("dp")
    half = HALF_TAPS * irp
    lane = lax.broadcasted_iota(jnp.int32, (half, 128), 1)
    for j in range(nd):
        target = lax.bitwise_xor(dp, j)
        moved = pltpu.roll(product, lax.rem(WIDE - target * ob, WIDE), 1)[:, :128]
        low = jnp.where(lane < ob, moved[:half], 0.0)
        high = jnp.where(lane < ob, moved[half:], 0.0)
        w_outs[j][...] = (low + roll(high, 64)).astype(w_outs[j].dtype)


def end_kernel(nc, ir, irp, channels, bias_ref, inside_ref, *refs):
    received, (conv_ref, grad_ref, blocks) = refs[:nc], refs[nc:]
    chip = place()[0]
    conv = received[0][:channels]
    for ref in received[1:]:
        conv = conv + ref[:channels].astype(F32)
    bias = bias_ref[...]
    conv = (conv + jnp.concatenate([bias, bias], axis=1)) * inside_ref[0:1]
    conv_ref[...] = conv.T.astype(BF16)
    for j in range(nc):
        blocks[lax.bitwise_xor(chip, j)] = received[j][channels:].astype(F32)
    parts = [blocks[q, core * irp : core * irp + ir] for q in range(nc) for core in range(2)]
    grad_ref[...] = jnp.concatenate(parts, axis=0).T.astype(BF16)


def weight_end_kernel(ir, irp, ob, *refs):
    w_refs, (weight_ref, total) = refs[:-2], refs[-2:]
    value = w_refs[0][...]
    for ref in w_refs[1:]:
        value = value + ref[...].astype(F32)
    total[...] = value
    for u in range(27):
        p, at = (u, 0) if u < HALF_TAPS else (u - HALF_TAPS, 64)
        weight_ref[u] = total[p * irp : p * irp + ir, at : at + ob]


def on_device(
    features, out_grad, weight, bias, gamma, beta, tile_clip, tile_rows, clip_cols, clip_start
):
    n, nd = lax.axis_size("tile"), lax.axis_size("dp")
    nc = n // 2
    channels = features.shape[-1]
    ir, _, ob = weight.shape
    irp = up(ir, 8)
    cbp = 2 * irp
    width = n * CELLS
    half = HALF_TAPS * irp
    smem = pl.BlockSpec(memory_space=pltpu.SMEM)
    vmem = pl.BlockSpec(memory_space=pltpu.VMEM)
    hbm = pl.BlockSpec(memory_space=pltpu.HBM)

    def shape(dims, dtype=BF16):
        return jax.ShapeDtypeStruct(dims, dtype)

    def call(kernel, args, out, scratch=(), specs=None, us=1.0, room=8, after=()):
        def body(*refs):
            kernel[0](*kernel[1:], *refs[: len(args)], *refs[len(args) + len(after) :])

        return pl.pallas_call(
            body,
            out_shape=out,
            in_specs=(specs or [vmem] * len(args)) + [hbm] * len(after),
            out_specs=jax.tree.map(lambda _: vmem, out),
            scratch_shapes=list(scratch),
            compiler_params=pltpu.CompilerParams(vmem_limit_bytes=room << 20),
            cost_estimate=pl.CostEstimate(flops=int(us * 1e9), bytes_accessed=0, transcendentals=0),
        )(*args, *after)

    def along_chips(x, j):
        return lax.ppermute(x, "tile", [(i, i ^ (2 * j)) for i in range(n)])

    def swap(x):
        return lax.ppermute(x, "tile", [(i, i ^ 1) for i in range(n)])

    def along_dp(x, j):
        return lax.ppermute(x, "dp", [(i, i ^ j) for i in range(nd)])

    packed_rows = 2 * cbp + CELLS + CELLS // 2
    taps_first = pltpu.with_memory_space_constraint(weight.transpose(1, 0, 2), pltpu.HBM)
    taps_other = swap(taps_first)
    sent = call(
        (prepare_kernel, nc, ir, irp),
        tuple(
            pltpu.with_memory_space_constraint(x.reshape(CELLS, channels), pltpu.HBM)
            for x in (features, out_grad)
        )
        + (taps_first,),
        [shape((packed_rows, 128))] * nc + [shape((27, ir, ob))],
        [
            pltpu.VMEM((CELLS, channels), BF16),
            pltpu.VMEM((CELLS, channels), BF16),
            pltpu.VMEM((nc, cbp, CELLS), F32),
            pltpu.SemaphoreType.DMA((3,)),
        ],
        [hbm] * 3,
    )
    sent, taps_first = sent[:nc], sent[nc]
    own = [sent[0]] + [along_chips(sent[j], j) for j in range(1, nc)]
    other = [swap(x) for x in own]
    w_block = call(
        (pack_kernel, ir, irp, ob),
        (taps_first, taps_other),
        shape((HALF_TAPS * cbp, 128)),
        [pltpu.VMEM((HALF_TAPS * cbp, 128), F32)],
    )
    w_blocks = [w_block] + [along_dp(w_block, j) for j in range(1, nd)]

    tables = (tile_clip, tile_rows, clip_cols, clip_start)
    lanes, rows, columns_, tiles, inside, bias_columns, picks, turned = call(
        (tables_kernel, n, nd, ir, irp, ob, channels),
        (*tables, gamma[None], beta[None], bias[None]),
        [
            shape((8, width), F32),
            shape((width, 128), F32),
            shape((2, cbp, 128), F32),
            shape((4, up(n, 8), 128), F32),
            shape((8, CELLS), F32),
            shape((channels, 128), F32),
            shape((2, nd * 128, WIDE)),
            shape((2, WIDE, nd * 128)),
        ],
        (),
        [smem] * 4 + [vmem] * 3,
        10.0,
    )
    conv_weight, grad_weight = call(
        (weight_kernel, nd, ir, irp, channels),
        (picks, turned, *w_blocks),
        [shape((3, channels, 9 * cbp)), shape((9 * cbp, 3 * WIDE))],
        us=10.0,
        after=(),
    )
    parts = call(
        (main_kernel, nc, nd, ir, irp, ob, channels),
        (lanes, rows, columns_, tiles, conv_weight, grad_weight, *own, *other),
        [shape((channels + cbp, CELLS), F32)]
        + [shape((channels + cbp, CELLS))] * (nc - 1)
        + [shape((width, WIDE)), shape((3, irp, width))],
        [
            pltpu.VMEM((n, cbp, CELLS), F32),
            pltpu.VMEM((n, CELLS, WIDE), F32),
            pltpu.VMEM((width, WIDE), BF16),
            pltpu.VMEM((width, WIDE), BF16),
            pltpu.VMEM((9 * cbp, nc * CELLS), BF16),
            pltpu.VMEM((nc, channels + cbp, CELLS), F32),
        ],
        None,
        5.0,
        16 + 5 * n // 4,
    )
    ends, centre, hidden = parts[:nc], parts[nc], parts[nc + 1]
    w_parts = call(
        (weight_grad_kernel, n, nd, irp, ob),
        (hidden, centre),
        [shape((half, 128), F32)] + [shape((half, 128))] * (nd - 1),
        [pltpu.VMEM((2 * half, width), BF16)],
        None,
        3.0,
        8 + n,
    )
    w_received = [w_parts[0]] + [along_dp(w_parts[j], j) for j in range(1, nd)]
    ends = [ends[0]] + [along_chips(ends[j], j) for j in range(1, nc)]
    conv_out, input_grad = call(
        (end_kernel, nc, ir, irp, channels),
        (bias_columns, inside, *ends),
        [shape((CELLS, channels)), shape((CELLS, channels))],
        [pltpu.VMEM((nc, cbp, CELLS), F32)],
    )
    weight_grad = call(
        (weight_end_kernel, ir, irp, ob),
        tuple(w_received),
        shape((27, ir, ob), F32),
        [pltpu.VMEM((half, 128), F32)],
        after=tuple(ends[1:-1]),
    )
    return (
        conv_out.reshape(features.shape),
        input_grad.reshape(features.shape),
        weight_grad.transpose(1, 0, 2),
    )


def solution(mesh):
    in_specs = (
        P("dp", None, "tile", None, None),
        P("dp", None, "tile", None, None),
        P("tile", None, "dp"),
        P(),
        P(),
        P(),
        P("dp", None),
        P("dp", None),
        P("dp", None),
        P("dp", None),
    )
    out_specs = (
        P("dp", None, "tile", None, None),
        P("dp", None, "tile", None, None),
        P("tile", None, "dp"),
    )
    return jax.shard_map(
        on_device, mesh=mesh, in_specs=in_specs, out_specs=out_specs, check_vma=False
    )
```

```python
import functools

import jax
import jax.numpy as jnp
from jax import lax
from jax.experimental import pallas as pl
from jax.experimental.pallas import tpu as pltpu
from jax.sharding import PartitionSpec as P

G = 32
EPSILON = 1e-05
WIDE = 256
HALF_TAPS = 14
FRAMES, HEIGHT, WIDTH = 4, 8, 8
CELLS = FRAMES * HEIGHT * WIDTH
BF16, F32 = jnp.bfloat16, jnp.float32
NT = (((1,), (1,)), ((), ()))

def up(value, multiple):
    return -(-value // multiple) * multiple


def roll(x, shift):
    size = x.shape[-1]
    shift = shift % size
    return pltpu.roll(x, shift, x.ndim - 1) if shift else x


def dot(x, y):
    return jnp.dot(x, y, preferred_element_type=F32)


def exact_dot(x, y):
    return jnp.dot(x, y, preferred_element_type=F32, precision=lax.Precision.HIGHEST)


def place():
    position = lax.axis_index("tile")
    core = lax.rem(position, 2)
    return lax.div(position, 2), core, core == 0


def cell_index(shape, axis):
    cell = lax.broadcasted_iota(jnp.int32, shape, axis)
    return (
        lax.shift_right_logical(cell, 6),
        lax.bitwise_and(lax.shift_right_logical(cell, 3), 7),
        lax.bitwise_and(cell, 7),
    )


def column(row_ref, channel_of, rows):
    channels = row_ref.shape[1]
    lane = lax.broadcasted_iota(jnp.int32, (rows, channels), 1)
    index = channel_of(lax.broadcasted_iota(jnp.int32, (rows, channels), 0))
    return jnp.sum(jnp.where(lane == index, row_ref[...], 0.0), axis=1, keepdims=True)


def block_row(index, real, padded):
    block = index // padded
    return block, index - block * padded


def prepare_kernel(nc, ir, irp, x_hbm, g_hbm, w_hbm, *rest):
    outs, (w_ref, x_ref, g_ref, blocks, sems) = rest[:nc], rest[nc:]
    cbp = 2 * irp
    copies = [
        pltpu.make_async_copy(src, dst, sems.at[i])
        for i, (src, dst) in enumerate(((x_hbm, x_ref), (g_hbm, g_ref), (w_hbm, w_ref)))
    ]
    for copy in copies:
        copy.start()
    chip = place()[0]
    if irp != ir:
        blocks[...] = jnp.zeros_like(blocks)
    copies[0].wait()
    turned = x_ref[...].astype(F32).T
    for q in range(nc):
        for core in range(2):
            at = (2 * q + core) * ir
            blocks[q, core * irp : core * irp + ir, :] = turned[at : at + ir]
    for j in range(nc):
        mine = blocks[lax.bitwise_xor(chip, j)].astype(BF16)
        outs[j][0:cbp] = mine[:, :128]
        outs[j][cbp : 2 * cbp] = mine[:, 128:]
    copies[1].wait()
    low = g_ref[:, :128]
    high = g_ref[:, 128:192].astype(F32)
    high = jnp.concatenate([high[: CELLS // 2], high[CELLS // 2 :]], axis=1).astype(BF16)
    for j in range(nc):
        outs[j][2 * cbp : 2 * cbp + CELLS] = low
        outs[j][2 * cbp + CELLS :] = high
    copies[2].wait()


def pack_kernel(ir, irp, ob, own_ref, other_ref, out_ref, packed):
    cbp = 2 * irp
    even = place()[2]
    packed[...] = jnp.zeros_like(packed)
    for u in range(27):
        p, start = (u, 0) if u < HALF_TAPS else (u - HALF_TAPS, 64)
        mine, theirs = own_ref[u].astype(F32), other_ref[u].astype(F32)
        at = p * cbp
        packed[at : at + ir, start : start + ob] = jnp.where(even, mine, theirs)
        packed[at + irp : at + irp + ir, start : start + ob] = jnp.where(even, theirs, mine)
    out_ref[...] = packed[...].astype(BF16)


def tables_kernel(n, nd, ir, irp, ob, channels, *refs):
    clip_ref, rows_ref, cols_ref, start_ref, gamma_ref, beta_ref, bias_ref = refs[:7]
    lanes_out, rows_out, columns_out, tiles_out, end_out, bias_out, pick_out, turned_out = refs[7:]
    group_size = channels // G
    cbp = 2 * irp
    chip = place()[0]
    position = lax.axis_index("tile")
    clip = [clip_ref[0, m] for m in range(n)]
    rows = [rows_ref[0, m] for m in range(n)]
    cols = [cols_ref[0, clip[m]] for m in range(n)]
    start = [start_ref[0, clip[m]] for m in range(n)]
    same = [[(clip[k] == clip[m]).astype(jnp.int32) for k in range(n)] for m in range(n)]
    above = [same[m][m - 1] if m else jnp.int32(0) for m in range(n)]
    below = [same[m][m + 1] if m < n - 1 else jnp.int32(0) for m in range(n)]

    def valid(m, f, r, c):
        return (f >= start[m]) & (r < rows[m]) & (c < cols[m])

    f, r, c = cell_index((1, CELLS), 1)
    lanes_out[...] = jnp.zeros_like(lanes_out)
    for m in range(n):
        at = slice(m * CELLS, (m + 1) * CELLS)
        lanes_out[0:1, at] = valid(m, f, r, c).astype(F32)
        lanes_out[1:2, at] = ((r > 0) | (above[m] > 0)).astype(F32)
        lanes_out[2:3, at] = ((r < 7) | (below[m] > 0)).astype(F32)
    own_clip = clip_ref[0, position]
    inside = (f >= start_ref[0, own_clip]) & (r < rows_ref[0, position]) & (c < cols_ref[0, own_clip])
    end_out[...] = jnp.broadcast_to(inside.astype(F32), end_out.shape)
    f, r, c = cell_index((CELLS, 128), 0)
    for m in range(n):
        rows_out[m * CELLS : (m + 1) * CELLS] = valid(m, f, r, c).astype(F32)
    lane = lax.broadcasted_iota(jnp.int32, (1, 128), 1)
    count = jnp.ones((1, 128), jnp.int32)
    tiles_out[...] = jnp.zeros_like(tiles_out)
    for m in range(n):
        clip_rows = jnp.int32(0)
        mates = jnp.zeros((1, 128), jnp.int32)
        for k in range(n):
            clip_rows += same[m][k] * rows[k]
            mates = jnp.where(lane == k, same[m][k], mates)
        cells = (FRAMES - start[m]) * cols[m] * clip_rows * group_size
        count = jnp.where(lane == m, cells, count)
        tiles_out[0, m : m + 1] = mates.astype(F32)
        tiles_out[1, m : m + 1] = jnp.full((1, 128), above[m]).astype(F32)
        tiles_out[2, m : m + 1] = jnp.full((1, 128), below[m]).astype(F32)
    tiles_out[3, 0:1] = count.astype(F32)

    def channel(index):
        block, inner = block_row(index, ir, irp)
        return jnp.where(inner < ir, chip * 2 * ir + block * ir + inner, -1)

    columns_out[0] = jnp.broadcast_to(column(gamma_ref, channel, cbp), (cbp, 128))
    columns_out[1] = jnp.broadcast_to(column(beta_ref, channel, cbp), (cbp, 128))
    bias_out[...] = jnp.broadcast_to(column(bias_ref, lambda index: index, channels), (channels, 128))
    dp = lax.axis_index("dp")
    for half, first in enumerate((0, 64)):
        for j in range(nd):
            base = lax.bitwise_xor(dp, j) * ob
            at = slice(j * 128, (j + 1) * 128)
            for dims, axis in (((128, WIDE), 1), ((WIDE, 128), 0)):
                lane = lax.broadcasted_iota(jnp.int32, dims, 1 - axis) - first
                out = lax.broadcasted_iota(jnp.int32, dims, axis) - base
                pick = ((lane == out) & (lane >= 0) & (lane < ob)).astype(F32).astype(BF16)
                if axis:
                    pick_out[half, at] = pick
                else:
                    turned_out[half, :, at] = pick


def weight_kernel(nd, ir, irp, channels, pick_ref, turned_ref, *refs):
    conv_out, grad_out = refs[nd:]
    cbp = 2 * irp
    joined = jnp.concatenate([ref[...] for ref in refs[:nd]], axis=1)
    low, high = (lax.dot_general(turned_ref[i], joined, NT, preferred_element_type=F32)[:channels] for i in range(2))
    frames = (
        low[:, : 9 * cbp],
        jnp.concatenate([low[:, 9 * cbp :], high[:, : 4 * cbp]], axis=1),
        high[:, 4 * cbp : 13 * cbp],
    )
    for a in range(3):
        conv_out[a] = frames[a].astype(BF16)
    straight = jnp.concatenate([dot(joined, pick_ref[i]) for i in range(2)], axis=0)
    for b in range(3):
        taps = [9 * a + 3 * b + e for a in range(3) for e in range(3)]
        part = jnp.concatenate([straight[t * cbp : (t + 1) * cbp] for t in taps], axis=0)
        grad_out[:, b * WIDE : (b + 1) * WIDE] = part.astype(BF16)


def row_neighbours(x, edges_ref):
    n = x.shape[1] // CELLS
    r = jnp.concatenate([cell_index((1, CELLS), 1)[1]] * n, axis=1)
    above = roll(jnp.where(r == 7, roll(x, CELLS - 64), x), 8) * edges_ref[1:2, :]
    below = roll(jnp.where(r == 0, roll(x, 64 - CELLS), x), -8) * edges_ref[2:3, :]
    return above, below


def columns(x, c):
    return jnp.where(c > 0, roll(x, 1), 0.0), x, jnp.where(c < 7, roll(x, -1), 0.0)


def later(x, f, late):
    return jnp.where(f >= late, roll(x, 64 * late), 0.0) if late else x


def main_kernel(nc, nd, ir, irp, ob, channels, *refs):
    n = 2 * nc
    cbp = 2 * irp
    width = n * CELLS
    group_size = channels // G
    lanes_ref, rows_ref, columns_ref, tiles_ref = refs[:4]
    conv_weight, grad_weight, refs = *refs[4:6], refs[6:]
    own, other, refs = refs[:nc], refs[nc:n], refs[n:]
    outs, refs = refs[:nc], refs[nc:]
    centre, hidden_out, features, grads, under, over, patches, ends = refs
    chip, core, even = place()
    lane = lax.broadcasted_iota(jnp.int32, (CELLS // 2, 128), 1)
    for j in range(nc):
        source = 2 * lax.bitwise_xor(chip, j)
        for m, ref in ((source + core, own[j]), (source + 1 - core, other[j])):
            features[m] = jnp.concatenate([ref[0:cbp], ref[cbp : 2 * cbp]], axis=1).astype(F32)
            low = ref[2 * cbp : 2 * cbp + CELLS].astype(F32)
            high = ref[2 * cbp + CELLS :].astype(F32)
            right = [jnp.where(lane < 64, high, 0.0), jnp.where(lane < 64, roll(high, 64), 0.0)]
            grads[m] = jnp.concatenate([low, jnp.concatenate(right, axis=0)], axis=1)
    gamma, beta = columns_ref[0][:, :1], columns_ref[1][:, :1]
    counted = tiles_ref[3, 0:1]

    def clip_totals(sums):
        total = jnp.zeros((cbp, 128), F32)
        for m in range(n):
            total = total + sums[m] * tiles_ref[0, m : m + 1]
        return total

    def group_of(axis):
        index = lax.broadcasted_iota(jnp.int32, (cbp, cbp), axis)
        block, inner = block_row(index, ir, irp)
        return jnp.where(inner < ir, (block * ir + inner) // group_size, -1 - index)

    groups = (group_of(0) == group_of(1)).astype(F32)
    valid, first, square = [], [], []
    for m in range(n):
        keep = lanes_ref[0:1, m * CELLS : (m + 1) * CELLS]
        block = features[m] * keep
        features[m] = block
        valid.append(keep)
        first.append(jnp.sum(block, axis=1, keepdims=True))
        square.append(jnp.sum(block * block, axis=1, keepdims=True))
    mean = exact_dot(groups, clip_totals(first)) / counted
    variance = exact_dot(groups, clip_totals(square)) / counted - mean * mean
    inv_std = lax.rsqrt(variance + EPSILON)

    def normed_of(m):
        return (features[m] - mean[:, m : m + 1]) * inv_std[:, m : m + 1]

    hidden = []
    for m in range(n):
        activation = normed_of(m) * gamma + beta
        hidden.append(activation * jax.nn.sigmoid(activation) * valid[m])
    hidden = jnp.concatenate(hidden, axis=1).astype(BF16).astype(F32)
    above, below = row_neighbours(hidden, lanes_ref)

    for b, x in enumerate((above, hidden, below)):
        hidden_out[b] = jnp.where(even, x[:irp], x[irp:]).astype(BF16)

    def own_tiles(x):
        parts = []
        for k in range(nc):
            low = x[:, 2 * k * CELLS : (2 * k + 1) * CELLS]
            high = x[:, (2 * k + 1) * CELLS : (2 * k + 2) * CELLS]
            parts.append(jnp.where(even, low, high))
        return jnp.concatenate(parts, axis=1)

    frame, _, col = cell_index((1, CELLS), 1)
    f, c = jnp.concatenate([frame] * nc, axis=1), jnp.concatenate([col] * nc, axis=1)
    for b, x in enumerate((above, hidden, below)):
        for e, block in enumerate(columns(own_tiles(x), c)):
            at = (3 * b + e) * cbp
            patches[at : at + cbp] = block.astype(BF16)
    total = jnp.zeros((channels, nc * CELLS), F32)
    for a in range(3):
        total = total + later(dot(conv_weight[a], patches[...]), f, 2 - a)
    for k in range(nc):
        ends[k, :channels] = total[:, k * CELLS : (k + 1) * CELLS]

    for m in range(n):
        keep = rows_ref[m * CELLS : (m + 1) * CELLS]
        grads[m] = grads[m] * jnp.concatenate([keep, keep], axis=1)
    split = (FRAMES, HEIGHT, WIDTH, WIDE)
    for m in range(n):
        here = grads[m]
        rows = here.reshape(split)
        has = [jnp.concatenate([tiles_ref[i, m : m + 1]] * 2, axis=1) for i in (1, 2)]
        last = grads[max(m - 1, 0)].reshape(split)[:, 7:] * has[0]
        next_ = grads[min(m + 1, n - 1)].reshape(split)[:, :1] * has[1]
        at = slice(m * CELLS, (m + 1) * CELLS)
        under[at] = jnp.concatenate([rows[:, 1:], next_], axis=1).reshape(CELLS, WIDE).astype(BF16)
        centre[at] = here.astype(BF16)
        over[at] = jnp.concatenate([last, rows[:, :7]], axis=1).reshape(CELLS, WIDE).astype(BF16)
    rows = jnp.concatenate([under[...], centre[...], over[...]], axis=1)
    total = lax.dot_general(grad_weight[...], rows, NT, preferred_element_type=F32)
    f, c = jnp.concatenate([frame] * n, axis=1), jnp.concatenate([col] * n, axis=1)
    hidden_grad = jnp.zeros((cbp, width), F32)
    for e in range(3):
        moved = jnp.zeros((cbp, width), F32)
        for a in range(3):
            late = 2 - a
            block = total[(3 * a + e) * cbp : (3 * a + e + 1) * cbp]
            moved = moved + (jnp.where(f < FRAMES - late, roll(block, -64 * late), 0.0) if late else block)
        if e == 0:
            moved = jnp.where(c < 7, roll(moved, -1), 0.0)
        elif e == 2:
            moved = jnp.where(c > 0, roll(moved, 1), 0.0)
        hidden_grad = hidden_grad + moved
    dnormed, first, second = [], [], []
    for m in range(n):
        norm = normed_of(m)
        activation = norm * gamma + beta
        s = jax.nn.sigmoid(activation)
        grad = hidden_grad[:, m * CELLS : (m + 1) * CELLS]
        grad = grad * valid[m] * s * (1.0 + activation * (1.0 - s)) * gamma
        dnormed.append(grad)
        first.append(jnp.sum(grad, axis=1, keepdims=True))
        second.append(jnp.sum(grad * norm, axis=1, keepdims=True))
    first_total = exact_dot(groups, clip_totals(first)) / counted
    second_total = exact_dot(groups, clip_totals(second)) / counted
    for k in range(nc):
        pair = []
        for m in (2 * k, 2 * k + 1):
            grad = dnormed[m] - first_total[:, m : m + 1] - normed_of(m) * second_total[:, m : m + 1]
            pair.append(grad * inv_std[:, m : m + 1] * valid[m])
        ends[k, channels:] = jnp.where(even, *pair)
    for j in range(nc):
        outs[j][...] = ends[lax.bitwise_xor(chip, j)].astype(outs[j].dtype)


def weight_grad_kernel(n, nd, irp, ob, hidden_ref, centre_ref, *refs):
    w_outs, patches = refs[:nd], refs[nd]
    cbp = 2 * irp
    frame, _, col = cell_index((1, CELLS), 1)
    f, c = jnp.concatenate([frame] * n, axis=1), jnp.concatenate([col] * n, axis=1)
    blocks = {}
    for b in range(3):
        for e, block in enumerate(columns(hidden_ref[b].astype(F32), c)):
            for a in range(3):
                blocks[9 * a + 3 * b + e] = later(block, f, 2 - a)
    blocks[27] = jnp.zeros_like(blocks[0])
    for p in range(HALF_TAPS):
        both = jnp.concatenate([blocks[2 * p], blocks[2 * p + 1]], axis=0)
        patches[p * cbp : (p + 1) * cbp] = both.astype(BF16)
    product = dot(patches[...], centre_ref[...])
    dp = lax.axis_index("dp")
    half = HALF_TAPS * irp
    lane = lax.broadcasted_iota(jnp.int32, (half, 128), 1)
    for j in range(nd):
        target = lax.bitwise_xor(dp, j)
        moved = pltpu.roll(product, lax.rem(WIDE - target * ob, WIDE), 1)[:, :128]
        low = jnp.where(lane < ob, moved[:half], 0.0)
        high = jnp.where(lane < ob, moved[half:], 0.0)
        w_outs[j][...] = (low + roll(high, 64)).astype(w_outs[j].dtype)


def end_kernel(nc, ir, irp, channels, bias_ref, inside_ref, *refs):
    received, (conv_ref, grad_ref, blocks) = refs[:nc], refs[nc:]
    chip = place()[0]
    conv = received[0][:channels]
    for ref in received[1:]:
        conv = conv + ref[:channels].astype(F32)
    bias = bias_ref[...]
    conv = (conv + jnp.concatenate([bias, bias], axis=1)) * inside_ref[0:1]
    conv_ref[...] = conv.T.astype(BF16)
    for j in range(nc):
        blocks[lax.bitwise_xor(chip, j)] = received[j][channels:].astype(F32)
    parts = [blocks[q, core * irp : core * irp + ir] for q in range(nc) for core in range(2)]
    grad_ref[...] = jnp.concatenate(parts, axis=0).T.astype(BF16)


def weight_end_kernel(ir, irp, ob, *refs):
    w_refs, (weight_ref, total) = refs[:-2], refs[-2:]
    value = w_refs[0][...]
    for ref in w_refs[1:]:
        value = value + ref[...].astype(F32)
    total[...] = value
    for u in range(27):
        p, at = (u, 0) if u < HALF_TAPS else (u - HALF_TAPS, 64)
        weight_ref[u] = total[p * irp : p * irp + ir, at : at + ob]


def on_device(
    features, out_grad, weight, bias, gamma, beta, tile_clip, tile_rows, clip_cols, clip_start
):
    n, nd = lax.axis_size("tile"), lax.axis_size("dp")
    nc = n // 2
    channels = features.shape[-1]
    ir, _, ob = weight.shape
    irp = up(ir, 8)
    cbp = 2 * irp
    width = n * CELLS
    half = HALF_TAPS * irp
    smem = pl.BlockSpec(memory_space=pltpu.SMEM)
    vmem = pl.BlockSpec(memory_space=pltpu.VMEM)
    hbm = pl.BlockSpec(memory_space=pltpu.HBM)

    def shape(dims, dtype=BF16):
        return jax.ShapeDtypeStruct(dims, dtype)

    def call(kernel, args, out, scratch=(), specs=None, us=1.0, room=8, after=()):
        def body(*refs):
            kernel[0](*kernel[1:], *refs[: len(args)], *refs[len(args) + len(after) :])

        return pl.pallas_call(
            body,
            out_shape=out,
            in_specs=(specs or [vmem] * len(args)) + [hbm] * len(after),
            out_specs=jax.tree.map(lambda _: vmem, out),
            scratch_shapes=list(scratch),
            compiler_params=pltpu.CompilerParams(vmem_limit_bytes=room << 20),
            cost_estimate=pl.CostEstimate(flops=int(us * 1e9), bytes_accessed=0, transcendentals=0),
        )(*args, *after)

    def along_chips(x, j):
        return lax.ppermute(x, "tile", [(i, i ^ (2 * j)) for i in range(n)])

    def swap(x):
        return lax.ppermute(x, "tile", [(i, i ^ 1) for i in range(n)])

    def along_dp(x, j):
        return lax.ppermute(x, "dp", [(i, i ^ j) for i in range(nd)])

    packed_rows = 2 * cbp + CELLS + CELLS // 2
    taps_first = pltpu.with_memory_space_constraint(weight.transpose(1, 0, 2), pltpu.HBM)
    sent = call(
        (prepare_kernel, nc, ir, irp),
        tuple(
            pltpu.with_memory_space_constraint(x.reshape(CELLS, channels), pltpu.HBM)
            for x in (features, out_grad)
        )
        + (taps_first,),
        [shape((packed_rows, 128))] * nc + [shape((27, ir, ob))],
        [
            pltpu.VMEM((CELLS, channels), BF16),
            pltpu.VMEM((CELLS, channels), BF16),
            pltpu.VMEM((nc, cbp, CELLS), F32),
            pltpu.SemaphoreType.DMA((3,)),
        ],
        [hbm] * 3,
    )
    sent, taps_first = sent[:nc], sent[nc]
    taps_other = swap(taps_first)
    own = [sent[0]] + [along_chips(sent[j], j) for j in range(1, nc)]
    other = [swap(x) for x in own]
    w_block = call(
        (pack_kernel, ir, irp, ob),
        (taps_first, taps_other),
        shape((HALF_TAPS * cbp, 128)),
        [pltpu.VMEM((HALF_TAPS * cbp, 128), F32)],
    )
    w_blocks = [w_block] + [along_dp(w_block, j) for j in range(1, nd)]

    tables = (tile_clip, tile_rows, clip_cols, clip_start)
    lanes, rows, columns_, tiles, inside, bias_columns, picks, turned = call(
        (tables_kernel, n, nd, ir, irp, ob, channels),
        (*tables, gamma[None], beta[None], bias[None]),
        [
            shape((8, width), F32),
            shape((width, 128), F32),
            shape((2, cbp, 128), F32),
            shape((4, up(n, 8), 128), F32),
            shape((8, CELLS), F32),
            shape((channels, 128), F32),
            shape((2, nd * 128, WIDE)),
            shape((2, WIDE, nd * 128)),
        ],
        (),
        [smem] * 4 + [vmem] * 3,
        10.0,
    )
    conv_weight, grad_weight = call(
        (weight_kernel, nd, ir, irp, channels),
        (picks, turned, *w_blocks),
        [shape((3, channels, 9 * cbp)), shape((9 * cbp, 3 * WIDE))],
        us=10.0,
        after=(),
    )
    parts = call(
        (main_kernel, nc, nd, ir, irp, ob, channels),
        (lanes, rows, columns_, tiles, conv_weight, grad_weight, *own, *other),
        [shape((channels + cbp, CELLS), F32)]
        + [shape((channels + cbp, CELLS))] * (nc - 1)
        + [shape((width, WIDE)), shape((3, irp, width))],
        [
            pltpu.VMEM((n, cbp, CELLS), F32),
            pltpu.VMEM((n, CELLS, WIDE), F32),
            pltpu.VMEM((width, WIDE), BF16),
            pltpu.VMEM((width, WIDE), BF16),
            pltpu.VMEM((9 * cbp, nc * CELLS), BF16),
            pltpu.VMEM((nc, channels + cbp, CELLS), F32),
        ],
        None,
        5.0,
        16 + 5 * n // 4,
    )
    ends, centre, hidden = parts[:nc], parts[nc], parts[nc + 1]
    w_parts = call(
        (weight_grad_kernel, n, nd, irp, ob),
        (hidden, centre),
        [shape((half, 128), F32)] + [shape((half, 128))] * (nd - 1),
        [pltpu.VMEM((2 * half, width), BF16)],
        None,
        3.0,
        8 + n,
    )
    w_received = [w_parts[0]] + [along_dp(w_parts[j], j) for j in range(1, nd)]
    ends = [ends[0]] + [along_chips(ends[j], j) for j in range(1, nc)]
    conv_out, input_grad = call(
        (end_kernel, nc, ir, irp, channels),
        (bias_columns, inside, *ends),
        [shape((CELLS, channels)), shape((CELLS, channels))],
        [pltpu.VMEM((nc, cbp, CELLS), F32)],
    )
    weight_grad = call(
        (weight_end_kernel, ir, irp, ob),
        tuple(w_received),
        shape((27, ir, ob), F32),
        [pltpu.VMEM((half, 128), F32)],
        after=tuple(ends[1:-1]),
    )
    return (
        conv_out.reshape(features.shape),
        input_grad.reshape(features.shape),
        weight_grad.transpose(1, 0, 2),
    )


def solution(mesh):
    in_specs = (
        P("dp", None, "tile", None, None),
        P("dp", None, "tile", None, None),
        P("tile", None, "dp"),
        P(),
        P(),
        P(),
        P("dp", None),
        P("dp", None),
        P("dp", None),
        P("dp", None),
    )
    out_specs = (
        P("dp", None, "tile", None, None),
        P("dp", None, "tile", None, None),
        P("tile", None, "dp"),
    )
    return jax.shard_map(
        on_device, mesh=mesh, in_specs=in_specs, out_specs=out_specs, check_vma=False
    )
```

```python
import functools

import jax
import jax.numpy as jnp
from jax import lax
from jax.experimental import pallas as pl
from jax.experimental.pallas import tpu as pltpu
from jax.sharding import PartitionSpec as P

G = 32
EPSILON = 1e-05
WIDE = 256
HALF_TAPS = 14
FRAMES, HEIGHT, WIDTH = 4, 8, 8
CELLS = FRAMES * HEIGHT * WIDTH
BF16, F32 = jnp.bfloat16, jnp.float32
NT = (((1,), (1,)), ((), ()))

def up(value, multiple):
    return -(-value // multiple) * multiple


def roll(x, shift):
    size = x.shape[-1]
    shift = shift % size
    return pltpu.roll(x, shift, x.ndim - 1) if shift else x


def dot(x, y):
    return jnp.dot(x, y, preferred_element_type=F32)


def exact_dot(x, y):
    return jnp.dot(x, y, preferred_element_type=F32, precision=lax.Precision.HIGHEST)


def place():
    position = lax.axis_index("tile")
    core = lax.rem(position, 2)
    return lax.div(position, 2), core, core == 0


def cell_index(shape, axis):
    cell = lax.broadcasted_iota(jnp.int32, shape, axis)
    return (
        lax.shift_right_logical(cell, 6),
        lax.bitwise_and(lax.shift_right_logical(cell, 3), 7),
        lax.bitwise_and(cell, 7),
    )


def column(row_ref, channel_of, rows):
    channels = row_ref.shape[1]
    lane = lax.broadcasted_iota(jnp.int32, (rows, channels), 1)
    index = channel_of(lax.broadcasted_iota(jnp.int32, (rows, channels), 0))
    return jnp.sum(jnp.where(lane == index, row_ref[...], 0.0), axis=1, keepdims=True)


def block_row(index, real, padded):
    block = index // padded
    return block, index - block * padded


def prepare_kernel(nc, ir, irp, x_hbm, g_hbm, w_hbm, *rest):
    outs, (w_ref, x_ref, g_ref, blocks, sems) = rest[:nc], rest[nc:]
    cbp = 2 * irp
    copies = [
        pltpu.make_async_copy(src, dst, sems.at[i])
        for i, (src, dst) in enumerate(((x_hbm, x_ref), (g_hbm, g_ref), (w_hbm, w_ref)))
    ]
    for copy in copies:
        copy.start()
    chip = place()[0]
    if irp != ir:
        blocks[...] = jnp.zeros_like(blocks)
    copies[0].wait()
    turned = x_ref[...].astype(F32).T
    for q in range(nc):
        for core in range(2):
            at = (2 * q + core) * ir
            blocks[q, core * irp : core * irp + ir, :] = turned[at : at + ir]
    for j in range(nc):
        mine = blocks[lax.bitwise_xor(chip, j)].astype(BF16)
        outs[j][0:cbp] = mine[:, :128]
        outs[j][cbp : 2 * cbp] = mine[:, 128:]
    copies[1].wait()
    low = g_ref[:, :128]
    high = g_ref[:, 128:192].astype(F32)
    high = jnp.concatenate([high[: CELLS // 2], high[CELLS // 2 :]], axis=1).astype(BF16)
    for j in range(nc):
        outs[j][2 * cbp : 2 * cbp + CELLS] = low
        outs[j][2 * cbp + CELLS :] = high
    copies[2].wait()


def pack_kernel(ir, irp, ob, own_ref, other_ref, out_ref, packed):
    cbp = 2 * irp
    even = place()[2]
    packed[...] = jnp.zeros_like(packed)
    for u in range(27):
        p, start = (u, 0) if u < HALF_TAPS else (u - HALF_TAPS, 64)
        mine, theirs = own_ref[u].astype(F32), other_ref[u].astype(F32)
        at = p * cbp
        packed[at : at + ir, start : start + ob] = jnp.where(even, mine, theirs)
        packed[at + irp : at + irp + ir, start : start + ob] = jnp.where(even, theirs, mine)
    out_ref[...] = packed[...].astype(BF16)


def tables_kernel(n, nd, ir, irp, ob, channels, *refs):
    clip_ref, rows_ref, cols_ref, start_ref, gamma_ref, beta_ref, bias_ref = refs[:7]
    lanes_out, rows_out, columns_out, tiles_out, end_out, bias_out, pick_out, turned_out = refs[7:]
    group_size = channels // G
    cbp = 2 * irp
    chip = place()[0]
    position = lax.axis_index("tile")
    clip = [clip_ref[0, m] for m in range(n)]
    rows = [rows_ref[0, m] for m in range(n)]
    cols = [cols_ref[0, clip[m]] for m in range(n)]
    start = [start_ref[0, clip[m]] for m in range(n)]
    same = [[(clip[k] == clip[m]).astype(jnp.int32) for k in range(n)] for m in range(n)]
    above = [same[m][m - 1] if m else jnp.int32(0) for m in range(n)]
    below = [same[m][m + 1] if m < n - 1 else jnp.int32(0) for m in range(n)]

    def valid(m, f, r, c):
        return (f >= start[m]) & (r < rows[m]) & (c < cols[m])

    f, r, c = cell_index((1, CELLS), 1)
    lanes_out[...] = jnp.zeros_like(lanes_out)
    for m in range(n):
        at = slice(m * CELLS, (m + 1) * CELLS)
        lanes_out[0:1, at] = valid(m, f, r, c).astype(F32)
        lanes_out[1:2, at] = ((r > 0) | (above[m] > 0)).astype(F32)
        lanes_out[2:3, at] = ((r < 7) | (below[m] > 0)).astype(F32)
    own_clip = clip_ref[0, position]
    inside = (f >= start_ref[0, own_clip]) & (r < rows_ref[0, position]) & (c < cols_ref[0, own_clip])
    end_out[...] = jnp.broadcast_to(inside.astype(F32), end_out.shape)
    f, r, c = cell_index((CELLS, 128), 0)
    for m in range(n):
        rows_out[m * CELLS : (m + 1) * CELLS] = valid(m, f, r, c).astype(F32)
    lane = lax.broadcasted_iota(jnp.int32, (1, 128), 1)
    count = jnp.ones((1, 128), jnp.int32)
    tiles_out[...] = jnp.zeros_like(tiles_out)
    for m in range(n):
        clip_rows = jnp.int32(0)
        mates = jnp.zeros((1, 128), jnp.int32)
        for k in range(n):
            clip_rows += same[m][k] * rows[k]
            mates = jnp.where(lane == k, same[m][k], mates)
        cells = (FRAMES - start[m]) * cols[m] * clip_rows * group_size
        count = jnp.where(lane == m, cells, count)
        tiles_out[0, m : m + 1] = mates.astype(F32)
        tiles_out[1, m : m + 1] = jnp.full((1, 128), above[m]).astype(F32)
        tiles_out[2, m : m + 1] = jnp.full((1, 128), below[m]).astype(F32)
    tiles_out[3, 0:1] = count.astype(F32)

    def channel(index):
        block, inner = block_row(index, ir, irp)
        return jnp.where(inner < ir, chip * 2 * ir + block * ir + inner, -1)

    columns_out[0] = jnp.broadcast_to(column(gamma_ref, channel, cbp), (cbp, 128))
    columns_out[1] = jnp.broadcast_to(column(beta_ref, channel, cbp), (cbp, 128))
    bias_out[...] = jnp.broadcast_to(column(bias_ref, lambda index: index, channels), (channels, 128))
    dp = lax.axis_index("dp")
    for half, first in enumerate((0, 64)):
        for j in range(nd):
            base = lax.bitwise_xor(dp, j) * ob
            at = slice(j * 128, (j + 1) * 128)
            for dims, axis in (((128, WIDE), 1), ((WIDE, 128), 0)):
                lane = lax.broadcasted_iota(jnp.int32, dims, 1 - axis) - first
                out = lax.broadcasted_iota(jnp.int32, dims, axis) - base
                pick = ((lane == out) & (lane >= 0) & (lane < ob)).astype(F32).astype(BF16)
                if axis:
                    pick_out[half, at] = pick
                else:
                    turned_out[half, :, at] = pick


def weight_kernel(nd, ir, irp, channels, pick_ref, turned_ref, *refs):
    conv_out, grad_out = refs[nd:]
    cbp = 2 * irp
    joined = jnp.concatenate([ref[...] for ref in refs[:nd]], axis=1)
    low, high = (lax.dot_general(turned_ref[i], joined, NT, preferred_element_type=F32)[:channels] for i in range(2))
    frames = (
        low[:, : 9 * cbp],
        jnp.concatenate([low[:, 9 * cbp :], high[:, : 4 * cbp]], axis=1),
        high[:, 4 * cbp : 13 * cbp],
    )
    for a in range(3):
        conv_out[a] = frames[a].astype(BF16)
    straight = jnp.concatenate([dot(joined, pick_ref[i]) for i in range(2)], axis=0)
    for b in range(3):
        taps = [9 * a + 3 * b + e for a in range(3) for e in range(3)]
        part = jnp.concatenate([straight[t * cbp : (t + 1) * cbp] for t in taps], axis=0)
        grad_out[:, b * WIDE : (b + 1) * WIDE] = part.astype(BF16)


def row_neighbours(x, edges_ref):
    n = x.shape[1] // CELLS
    r = jnp.concatenate([cell_index((1, CELLS), 1)[1]] * n, axis=1)
    above = roll(jnp.where(r == 7, roll(x, CELLS - 64), x), 8) * edges_ref[1:2, :]
    below = roll(jnp.where(r == 0, roll(x, 64 - CELLS), x), -8) * edges_ref[2:3, :]
    return above, below


def columns(x, c):
    return jnp.where(c > 0, roll(x, 1), 0.0), x, jnp.where(c < 7, roll(x, -1), 0.0)


def later(x, f, late):
    return jnp.where(f >= late, roll(x, 64 * late), 0.0) if late else x


def main_kernel(nc, nd, ir, irp, ob, channels, *refs):
    n = 2 * nc
    cbp = 2 * irp
    width = n * CELLS
    group_size = channels // G
    lanes_ref, rows_ref, columns_ref, tiles_ref = refs[:4]
    conv_weight, grad_weight, refs = *refs[4:6], refs[6:]
    own, other, refs = refs[:nc], refs[nc:n], refs[n:]
    outs, refs = refs[:nc], refs[nc:]
    centre, hidden_out, features, grads, under, over, patches, ends = refs
    chip, core, even = place()
    lane = lax.broadcasted_iota(jnp.int32, (CELLS // 2, 128), 1)
    for j in range(nc):
        source = 2 * lax.bitwise_xor(chip, j)
        for m, ref in ((source + core, own[j]), (source + 1 - core, other[j])):
            features[m] = jnp.concatenate([ref[0:cbp], ref[cbp : 2 * cbp]], axis=1).astype(F32)
            low = ref[2 * cbp : 2 * cbp + CELLS].astype(F32)
            high = ref[2 * cbp + CELLS :].astype(F32)
            right = [jnp.where(lane < 64, high, 0.0), jnp.where(lane < 64, roll(high, 64), 0.0)]
            keep = rows_ref[pl.ds(pl.multiple_of(m * CELLS, CELLS), CELLS)]
            grads[m] = jnp.concatenate([low * keep, jnp.concatenate(right, axis=0) * keep], axis=1)
    gamma, beta = columns_ref[0][:, :1], columns_ref[1][:, :1]
    counted = tiles_ref[3, 0:1]

    def clip_totals(sums):
        total = jnp.zeros((cbp, 128), F32)
        for m in range(n):
            total = total + sums[m] * tiles_ref[0, m : m + 1]
        return total

    def group_of(axis):
        index = lax.broadcasted_iota(jnp.int32, (cbp, cbp), axis)
        block, inner = block_row(index, ir, irp)
        return jnp.where(inner < ir, (block * ir + inner) // group_size, -1 - index)

    groups = (group_of(0) == group_of(1)).astype(F32)
    valid, first, square = [], [], []
    for m in range(n):
        keep = lanes_ref[0:1, m * CELLS : (m + 1) * CELLS]
        block = features[m] * keep
        features[m] = block
        valid.append(keep)
        first.append(jnp.sum(block, axis=1, keepdims=True))
        square.append(jnp.sum(block * block, axis=1, keepdims=True))
    mean = exact_dot(groups, clip_totals(first)) / counted
    variance = exact_dot(groups, clip_totals(square)) / counted - mean * mean
    inv_std = lax.rsqrt(variance + EPSILON)

    def normed_of(m):
        return (features[m] - mean[:, m : m + 1]) * inv_std[:, m : m + 1]

    hidden = []
    for m in range(n):
        activation = normed_of(m) * gamma + beta
        hidden.append(activation * jax.nn.sigmoid(activation) * valid[m])
    hidden = jnp.concatenate(hidden, axis=1).astype(BF16).astype(F32)
    above, below = row_neighbours(hidden, lanes_ref)

    for b, x in enumerate((above, hidden, below)):
        hidden_out[b] = jnp.where(even, x[:irp], x[irp:]).astype(BF16)

    def own_tiles(x):
        parts = []
        for k in range(nc):
            low = x[:, 2 * k * CELLS : (2 * k + 1) * CELLS]
            high = x[:, (2 * k + 1) * CELLS : (2 * k + 2) * CELLS]
            parts.append(jnp.where(even, low, high))
        return jnp.concatenate(parts, axis=1)

    frame, _, col = cell_index((1, CELLS), 1)
    f, c = jnp.concatenate([frame] * nc, axis=1), jnp.concatenate([col] * nc, axis=1)
    for b, x in enumerate((above, hidden, below)):
        for e, block in enumerate(columns(own_tiles(x), c)):
            at = (3 * b + e) * cbp
            patches[at : at + cbp] = block.astype(BF16)
    total = jnp.zeros((channels, nc * CELLS), F32)
    for a in range(3):
        total = total + later(dot(conv_weight[a], patches[...]), f, 2 - a)
    for k in range(nc):
        ends[k, :channels] = total[:, k * CELLS : (k + 1) * CELLS]

    split = (FRAMES, HEIGHT, WIDTH, WIDE)
    for m in range(n):
        here = grads[m]
        rows = here.reshape(split)
        has = [jnp.concatenate([tiles_ref[i, m : m + 1]] * 2, axis=1) for i in (1, 2)]
        last = grads[max(m - 1, 0)].reshape(split)[:, 7:] * has[0]
        next_ = grads[min(m + 1, n - 1)].reshape(split)[:, :1] * has[1]
        at = slice(m * CELLS, (m + 1) * CELLS)
        under[at] = jnp.concatenate([rows[:, 1:], next_], axis=1).reshape(CELLS, WIDE).astype(BF16)
        centre[at] = here.astype(BF16)
        over[at] = jnp.concatenate([last, rows[:, :7]], axis=1).reshape(CELLS, WIDE).astype(BF16)
    rows = jnp.concatenate([under[...], centre[...], over[...]], axis=1)
    total = lax.dot_general(grad_weight[...], rows, NT, preferred_element_type=F32)
    f, c = jnp.concatenate([frame] * n, axis=1), jnp.concatenate([col] * n, axis=1)
    hidden_grad = jnp.zeros((cbp, width), F32)
    for e in range(3):
        moved = jnp.zeros((cbp, width), F32)
        for a in range(3):
            late = 2 - a
            block = total[(3 * a + e) * cbp : (3 * a + e + 1) * cbp]
            moved = moved + (jnp.where(f < FRAMES - late, roll(block, -64 * late), 0.0) if late else block)
        if e == 0:
            moved = jnp.where(c < 7, roll(moved, -1), 0.0)
        elif e == 2:
            moved = jnp.where(c > 0, roll(moved, 1), 0.0)
        hidden_grad = hidden_grad + moved
    dnormed, first, second = [], [], []
    for m in range(n):
        norm = normed_of(m)
        activation = norm * gamma + beta
        s = jax.nn.sigmoid(activation)
        grad = hidden_grad[:, m * CELLS : (m + 1) * CELLS]
        grad = grad * valid[m] * s * (1.0 + activation * (1.0 - s)) * gamma
        dnormed.append(grad)
        first.append(jnp.sum(grad, axis=1, keepdims=True))
        second.append(jnp.sum(grad * norm, axis=1, keepdims=True))
    first_total = exact_dot(groups, clip_totals(first)) / counted
    second_total = exact_dot(groups, clip_totals(second)) / counted
    for k in range(nc):
        pair = []
        for m in (2 * k, 2 * k + 1):
            grad = dnormed[m] - first_total[:, m : m + 1] - normed_of(m) * second_total[:, m : m + 1]
            pair.append(grad * inv_std[:, m : m + 1] * valid[m])
        ends[k, channels:] = jnp.where(even, *pair)
    for j in range(nc):
        outs[j][...] = ends[lax.bitwise_xor(chip, j)].astype(outs[j].dtype)


def weight_grad_kernel(n, nd, irp, ob, hidden_ref, centre_ref, *refs):
    w_outs, patches = refs[:nd], refs[nd]
    cbp = 2 * irp
    frame, _, col = cell_index((1, CELLS), 1)
    f, c = jnp.concatenate([frame] * n, axis=1), jnp.concatenate([col] * n, axis=1)
    blocks = {}
    for b in range(3):
        for e, block in enumerate(columns(hidden_ref[b].astype(F32), c)):
            for a in range(3):
                blocks[9 * a + 3 * b + e] = later(block, f, 2 - a)
    blocks[27] = jnp.zeros_like(blocks[0])
    for p in range(HALF_TAPS):
        both = jnp.concatenate([blocks[2 * p], blocks[2 * p + 1]], axis=0)
        patches[p * cbp : (p + 1) * cbp] = both.astype(BF16)
    product = dot(patches[...], centre_ref[...])
    dp = lax.axis_index("dp")
    half = HALF_TAPS * irp
    lane = lax.broadcasted_iota(jnp.int32, (half, 128), 1)
    for j in range(nd):
        target = lax.bitwise_xor(dp, j)
        moved = pltpu.roll(product, lax.rem(WIDE - target * ob, WIDE), 1)[:, :128]
        low = jnp.where(lane < ob, moved[:half], 0.0)
        high = jnp.where(lane < ob, moved[half:], 0.0)
        w_outs[j][...] = (low + roll(high, 64)).astype(w_outs[j].dtype)


def end_kernel(nc, ir, irp, channels, bias_ref, inside_ref, *refs):
    received, (conv_ref, grad_ref, blocks) = refs[:nc], refs[nc:]
    chip = place()[0]
    conv = received[0][:channels]
    for ref in received[1:]:
        conv = conv + ref[:channels].astype(F32)
    bias = bias_ref[...]
    conv = (conv + jnp.concatenate([bias, bias], axis=1)) * inside_ref[0:1]
    conv_ref[...] = conv.T.astype(BF16)
    for j in range(nc):
        blocks[lax.bitwise_xor(chip, j)] = received[j][channels:].astype(F32)
    parts = [blocks[q, core * irp : core * irp + ir] for q in range(nc) for core in range(2)]
    grad_ref[...] = jnp.concatenate(parts, axis=0).T.astype(BF16)


def weight_end_kernel(ir, irp, ob, *refs):
    w_refs, (weight_ref, total) = refs[:-2], refs[-2:]
    value = w_refs[0][...]
    for ref in w_refs[1:]:
        value = value + ref[...].astype(F32)
    total[...] = value
    for u in range(27):
        p, at = (u, 0) if u < HALF_TAPS else (u - HALF_TAPS, 64)
        weight_ref[u] = total[p * irp : p * irp + ir, at : at + ob]


def on_device(
    features, out_grad, weight, bias, gamma, beta, tile_clip, tile_rows, clip_cols, clip_start
):
    n, nd = lax.axis_size("tile"), lax.axis_size("dp")
    nc = n // 2
    channels = features.shape[-1]
    ir, _, ob = weight.shape
    irp = up(ir, 8)
    cbp = 2 * irp
    width = n * CELLS
    half = HALF_TAPS * irp
    smem = pl.BlockSpec(memory_space=pltpu.SMEM)
    vmem = pl.BlockSpec(memory_space=pltpu.VMEM)
    hbm = pl.BlockSpec(memory_space=pltpu.HBM)

    def shape(dims, dtype=BF16):
        return jax.ShapeDtypeStruct(dims, dtype)

    def call(kernel, args, out, scratch=(), specs=None, us=1.0, room=8, after=()):
        def body(*refs):
            kernel[0](*kernel[1:], *refs[: len(args)], *refs[len(args) + len(after) :])

        return pl.pallas_call(
            body,
            out_shape=out,
            in_specs=(specs or [vmem] * len(args)) + [hbm] * len(after),
            out_specs=jax.tree.map(lambda _: vmem, out),
            scratch_shapes=list(scratch),
            compiler_params=pltpu.CompilerParams(vmem_limit_bytes=room << 20),
            cost_estimate=pl.CostEstimate(flops=int(us * 1e9), bytes_accessed=0, transcendentals=0),
        )(*args, *after)

    def along_chips(x, j):
        return lax.ppermute(x, "tile", [(i, i ^ (2 * j)) for i in range(n)])

    def swap(x):
        return lax.ppermute(x, "tile", [(i, i ^ 1) for i in range(n)])

    def along_dp(x, j):
        return lax.ppermute(x, "dp", [(i, i ^ j) for i in range(nd)])

    packed_rows = 2 * cbp + CELLS + CELLS // 2
    taps_first = pltpu.with_memory_space_constraint(weight.transpose(1, 0, 2), pltpu.HBM)
    sent = call(
        (prepare_kernel, nc, ir, irp),
        tuple(
            pltpu.with_memory_space_constraint(x.reshape(CELLS, channels), pltpu.HBM)
            for x in (features, out_grad)
        )
        + (taps_first,),
        [shape((packed_rows, 128))] * nc + [shape((27, ir, ob))],
        [
            pltpu.VMEM((CELLS, channels), BF16),
            pltpu.VMEM((CELLS, channels), BF16),
            pltpu.VMEM((nc, cbp, CELLS), F32),
            pltpu.SemaphoreType.DMA((3,)),
        ],
        [hbm] * 3,
    )
    sent, taps_first = sent[:nc], sent[nc]
    taps_other = swap(taps_first)
    own = [sent[0]] + [along_chips(sent[j], j) for j in range(1, nc)]
    other = [swap(x) for x in own]
    w_block = call(
        (pack_kernel, ir, irp, ob),
        (taps_first, taps_other),
        shape((HALF_TAPS * cbp, 128)),
        [pltpu.VMEM((HALF_TAPS * cbp, 128), F32)],
    )
    w_blocks = [w_block] + [along_dp(w_block, j) for j in range(1, nd)]

    tables = (tile_clip, tile_rows, clip_cols, clip_start)
    lanes, rows, columns_, tiles, inside, bias_columns, picks, turned = call(
        (tables_kernel, n, nd, ir, irp, ob, channels),
        (*tables, gamma[None], beta[None], bias[None]),
        [
            shape((8, width), F32),
            shape((width, 128), F32),
            shape((2, cbp, 128), F32),
            shape((4, up(n, 8), 128), F32),
            shape((8, CELLS), F32),
            shape((channels, 128), F32),
            shape((2, nd * 128, WIDE)),
            shape((2, WIDE, nd * 128)),
        ],
        (),
        [smem] * 4 + [vmem] * 3,
        10.0,
    )
    conv_weight, grad_weight = call(
        (weight_kernel, nd, ir, irp, channels),
        (picks, turned, *w_blocks),
        [shape((3, channels, 9 * cbp)), shape((9 * cbp, 3 * WIDE))],
        us=10.0,
        after=(),
    )
    parts = call(
        (main_kernel, nc, nd, ir, irp, ob, channels),
        (lanes, rows, columns_, tiles, conv_weight, grad_weight, *own, *other),
        [shape((channels + cbp, CELLS), F32)]
        + [shape((channels + cbp, CELLS))] * (nc - 1)
        + [shape((width, WIDE)), shape((3, irp, width))],
        [
            pltpu.VMEM((n, cbp, CELLS), F32),
            pltpu.VMEM((n, CELLS, WIDE), F32),
            pltpu.VMEM((width, WIDE), BF16),
            pltpu.VMEM((width, WIDE), BF16),
            pltpu.VMEM((9 * cbp, nc * CELLS), BF16),
            pltpu.VMEM((nc, channels + cbp, CELLS), F32),
        ],
        None,
        5.0,
        16 + 5 * n // 4,
    )
    ends, centre, hidden = parts[:nc], parts[nc], parts[nc + 1]
    w_parts = call(
        (weight_grad_kernel, n, nd, irp, ob),
        (hidden, centre),
        [shape((half, 128), F32)] + [shape((half, 128))] * (nd - 1),
        [pltpu.VMEM((2 * half, width), BF16)],
        None,
        3.0,
        8 + n,
    )
    w_received = [w_parts[0]] + [along_dp(w_parts[j], j) for j in range(1, nd)]
    ends = [ends[0]] + [along_chips(ends[j], j) for j in range(1, nc)]
    conv_out, input_grad = call(
        (end_kernel, nc, ir, irp, channels),
        (bias_columns, inside, *ends),
        [shape((CELLS, channels)), shape((CELLS, channels))],
        [pltpu.VMEM((nc, cbp, CELLS), F32)],
    )
    weight_grad = call(
        (weight_end_kernel, ir, irp, ob),
        tuple(w_received),
        shape((27, ir, ob), F32),
        [pltpu.VMEM((half, 128), F32)],
        after=tuple(ends[1:-1]),
    )
    return (
        conv_out.reshape(features.shape),
        input_grad.reshape(features.shape),
        weight_grad.transpose(1, 0, 2),
    )


def solution(mesh):
    in_specs = (
        P("dp", None, "tile", None, None),
        P("dp", None, "tile", None, None),
        P("tile", None, "dp"),
        P(),
        P(),
        P(),
        P("dp", None),
        P("dp", None),
        P("dp", None),
        P("dp", None),
    )
    out_specs = (
        P("dp", None, "tile", None, None),
        P("dp", None, "tile", None, None),
        P("tile", None, "dp"),
    )
    return jax.shard_map(
        on_device, mesh=mesh, in_specs=in_specs, out_specs=out_specs, check_vma=False
    )
```
